32 devices in a mesh: dp: 4 (over x, core), expert: 8 (over z, y).
Axes of the slice: x: 2, y: 2, z: 4, core: 2. Of those that a mesh axis runs over, the one named last changes fastest.
Arguments:
- tokens: bfloat16 [16384, 768], P(('dp', 'expert')), may hold values from -6 to 6
- cotangent: bfloat16 [16384, 768], P(('dp', 'expert')), may hold values from -6 to 6
- expert_ids: int32 [16384, 1], P(('dp', 'expert')), may hold values from 0 to 7
- loss_weights: int32 [8], replicated, may hold values from 1 to 4
- section: int32 [8], replicated, may hold values from 0 to 1, as said below
- norm_gains: float32 [4, 768], replicated, may hold values from 0.5 to 1.5
- attn_qkv: bfloat16 [2, 768, 2304], replicated, may hold values from -0.21875 to 0.21875
- attn_out: bfloat16 [2, 768, 768], replicated, may hold values from -1.25 to 1.25
- ffn_up: bfloat16 [768, 3072], replicated, may hold values from -0.21875 to 0.21875
- ffn_down: bfloat16 [3072, 768], replicated, may hold values from -0.21875 to 0.21875
- expert_up: bfloat16 [8, 768, 3072], P('expert'), may hold values from -0.21875 to 0.21875
- expert_down: bfloat16 [8, 3072, 768], P('expert'), may hold values from -0.3125 to 0.3125
- router: float32 [768, 8], replicated, may hold values from -0.15625 to 0.15625
Outputs:
- block_one: bfloat16 [16384, 768], P(('dp', 'expert'))
- block_two: bfloat16 [16384, 768], P(('dp', 'expert'))
- input_grad: float32 [16384, 768], P(('dp', 'expert'))
- balance_loss: float32 [], replicated
- gains_grad: float32 [4, 768], replicated
- qkv_grad: float32 [2, 768, 2304], P(None, 'expert')
- out_grad: float32 [2, 768, 768], P(None, 'expert')
- up_grad: float32 [768, 3072], P('expert')
- down_grad: float32 [3072, 768], P('expert')
- expert_up_grad: float32 [8, 768, 3072], P('expert', 'dp')
- expert_down_grad: float32 [8, 3072, 768], P('expert', 'dp')
- router_grad: float32 [768, 8], replicated
The draws below stay inside these ranges and needn't reach their ends.
Inputs may be any that keep to these rules, and one draw needn't show every extreme that they name: `expert_ids`: every expert is named by some token. `section`: some sequences have 0 and some have 1.
All inputs are finite; a program needn't handle non-finite values.
Results may differ from the reference program's by a relative error of at most 0.02.
Values may be sent and summed in bfloat16 or wider, within the bound.
A program may use at most 704 MiB of HBM per device.

```python
from functools import partial
import jax
import jax.numpy as jnp
from jax import lax

D = 768
H = 12
HD = 64
FF = 3072
TOK_DEV = 512
SEQ_LEN = 2048
EXPERTS = 8
CAP = 80
TOKENS = 16384
SEQS = 8
N_DP = 4
N_EXPERT = 8


def draw_section(key, part):
    key = jax.random.fold_in(key, 7)
    first_key, second_key, third_key = jax.random.split(key, 3)
    flags = jax.random.randint(first_key, (SEQS,), 0, 2, dtype=jnp.int32)
    zero_place = jax.random.randint(second_key, (), 0, SEQS, dtype=jnp.int32)
    offset = jax.random.randint(third_key, (), 1, SEQS, dtype=jnp.int32)
    one_place = (zero_place + offset) % SEQS
    flags = flags.at[zero_place].set(0)
    flags = flags.at[one_place].set(1)
    return flags


def set_ends(values, own_key, low, high):
    longest = values.shape.index(max(values.shape))
    spots = []
    for shift in (0, 1):
        where = [jax.random.randint(jax.random.fold_in(own_key, axis), (), 0, length) for axis, length in enumerate(values.shape)]
        where[longest] = (where[longest] + shift) % values.shape[longest]
        spots.append(tuple(where))
    return values.at[spots[0]].set(low).at[spots[1]].set(high)


def level_of(key, extent, cuts, smallest, high):
    factor_of = 1.0
    for dim, shards_of in cuts:
        draws = jax.random.uniform(jax.random.fold_in(jax.random.fold_in(key, 6), dim), (shards_of,), jnp.float32, smallest / len(cuts), high / len(cuts))
        factor_of = factor_of * jnp.repeat(jnp.exp(draws), extent[dim] // shards_of).reshape((-1,) + (1,) * (len(extent) - 1 - dim))
    return factor_of


def picks_of(stream_key, rows, amount, top, lift):
    ranking = jax.random.permutation(jax.random.fold_in(stream_key, 1), amount)
    favour = ranking
    for power in range(3):
        favour = favour * favour // amount
    favour = favour * lift // amount
    lots = jax.random.randint(jax.random.fold_in(stream_key, 2), (rows, amount), 0, 4096) + favour
    sure = jax.random.permutation(jax.random.fold_in(stream_key, 3), rows)[jnp.arange(amount) % rows]
    lots = jnp.where(jnp.arange(rows)[:, None] == sure[None, :], 1 << 14, lots)
    priority = lots * amount + jnp.arange(amount)
    return lax.top_k(priority.astype(jnp.int32), top)[1].astype(jnp.int32)


def noise(key, dims, deviation, limit, shards=(), held_as=jnp.bfloat16):
    result = jax.random.normal(key, dims, jnp.float32) * deviation
    if len(shards) > 0:
        result = level_of(key, dims, shards, -0.22, 0.18) * result
    return jnp.clip(result, min=-limit, max=limit).astype(held_as)


def setup_inputs(seed: int = 0) -> dict:
    seeds = jax.random.split(jax.random.key(seed), 14)
    tokens = noise(seeds[0], (TOKENS, D), 1.0, 6.0, ((0, 32),))
    cotangent = noise(seeds[1], (TOKENS, D), 1.0, 6.0, ((0, 32),))
    expert_ids = picks_of(seeds[2], TOKENS, EXPERTS, 1, 1024)
    loss_weights = set_ends(jax.random.randint(seeds[3], (SEQS,), 1, 5), jax.random.fold_in(seeds[3], 1), 1, 4).astype(jnp.int32)
    section = draw_section(jax.random.fold_in(seeds[13], 71), 0)
    norm_gains = jnp.clip(1.0 + 0.1 * jax.random.normal(seeds[5], (4, D), jnp.float32), 0.5, 1.5)
    attn_qkv = noise(seeds[6], (2, D, 3 * D), D ** -0.5, 0.21875)
    attn_out = noise(seeds[7], (2, D, D), (D // 32) ** -0.5, 1.25)
    ffn_up = noise(seeds[8], (D, FF), D ** -0.5, 0.21875)
    ffn_down = noise(seeds[9], (FF, D), (FF // 4) ** -0.5, 0.21875)
    expert_up = noise(seeds[10], (EXPERTS, D, FF), D ** -0.5, 0.21875, ((0, 8),))
    expert_down = noise(seeds[11], (EXPERTS, FF, D), (FF // 8) ** -0.5, 0.3125, ((0, 8),))
    router = noise(seeds[12], (D, EXPERTS), (2 * D) ** -0.5, 0.15625, (), jnp.float32)
    return dict(tokens=tokens, cotangent=cotangent, expert_ids=expert_ids, loss_weights=loss_weights, section=section, norm_gains=norm_gains, attn_qkv=attn_qkv, attn_out=attn_out, ffn_up=ffn_up, ffn_down=ffn_down, expert_up=expert_up, expert_down=expert_down, router=router)


@jax.custom_vjp
def low(v):
    return lax.optimization_barrier(v.astype(jnp.bfloat16)).astype(jnp.float32)

@jax.custom_vjp
def low_back(v):
    return v

def low_keep(v):
    return (low(v), None)

def low_pass(kept, grad):
    return (grad,)

def back_keep(v):
    return (v, None)

def back_low(kept, grad):
    return (low(grad),)
low.defvjp(low_keep, low_pass)
low_back.defvjp(back_keep, back_low)
highest = lax.Precision.HIGHEST
eps_norm = 1e-05
balance_rate = 1.0

def layer_norm(stream, gain):
    centre = lax.optimization_barrier(jnp.mean(stream, axis=-1, keepdims=True))
    centered = stream - centre
    spread = lax.optimization_barrier(jnp.mean(centered * centered, axis=-1, keepdims=True))
    return centered * lax.rsqrt(spread + eps_norm) * gain

def gelu_tanh(hidden):
    return jax.nn.gelu(hidden, approximate=True)

def attention(stream, gain, w_qkv, w_out):
    length = stream.shape[0]
    normed = low(layer_norm(stream, gain))
    packed = low(low_back(jnp.dot(normed, w_qkv, precision=highest)))
    queries = packed[:, :D].reshape(length, H, HD)
    keys = packed[:, D:2 * D].reshape(length, H, HD)
    values = packed[:, 2 * D:].reshape(length, H, HD)
    rows_block = min(512, length)
    key_place = jnp.arange(length)

    def one_block(first):
        query_rows = lax.dynamic_slice_in_dim(queries, first, rows_block, 0)
        scores = low_back(jnp.einsum('qhd,khd->hqk', query_rows, keys, precision=highest) * HD ** (-0.5))
        query_place = first + jnp.arange(rows_block)
        allowed = key_place[None, :] <= query_place[:, None]
        scores = jnp.where(allowed[None], scores, -1e+30)
        largest = lax.optimization_barrier(jnp.max(scores, axis=-1, keepdims=True))
        weights = jnp.exp(scores - largest)
        probs = weights / lax.optimization_barrier(jnp.sum(weights, axis=-1, keepdims=True))
        return jnp.einsum('hqk,khd->qhd', low(probs), values, precision=highest)
    starts = (jnp.arange(length // rows_block) * rows_block).astype(jnp.int32)
    mixed = lax.map(jax.checkpoint(one_block), starts).reshape(length, D)
    mixed = low(low_back(mixed))
    return low_back(jnp.dot(mixed, w_out, precision=highest))

def routing(expert_index):
    blocks = expert_index.reshape(-1, TOK_DEV)
    one_hot = (blocks[:, :, None] == jnp.arange(EXPERTS, dtype=jnp.int32)[None, None, :]).astype(jnp.int32)
    earlier = jnp.cumsum(one_hot, axis=1) - one_hot
    slots = lax.optimization_barrier(jnp.sum(earlier * one_hot, axis=-1)).astype(jnp.int32)
    kept_rows = slots < CAP
    target = jnp.where(kept_rows, blocks * CAP + slots, EXPERTS * CAP).astype(jnp.int32)
    return (target, kept_rows)

def expert_layer(rows, expert_index, w_up, w_down):
    target, kept_rows = routing(expert_index)
    count_blocks = target.shape[0]
    slots_all = EXPERTS * CAP

    def fill(block_rows, block_target):
        return jnp.zeros((slots_all, D), rows.dtype).at[block_target].add(block_rows, mode='drop')
    buffers = jax.vmap(fill)(rows.reshape(count_blocks, TOK_DEV, D), target)
    buffers = buffers.reshape(count_blocks, EXPERTS, CAP, D)
    hidden = low_back(jnp.einsum('becd,edf->becf', buffers, w_up, precision=highest))
    acts = low(gelu_tanh(hidden))
    outs = low(low_back(jnp.einsum('becf,efd->becd', acts, w_down, precision=highest)))
    outs = outs.reshape(count_blocks, slots_all, D)

    def pick(block_outs, block_target):
        return block_outs[jnp.minimum(block_target, slots_all - 1)]
    picked = jax.vmap(pick)(outs, target).reshape(-1, D)
    return picked * kept_rows.reshape(-1, 1).astype(rows.dtype)

def forward(params, inputs, expert_index):
    gains, qkv_w, out_w, up_w, down_w, e_up, e_down, router_w = params
    first_stream = inputs + attention(inputs, gains[0], qkv_w[0], out_w[0])
    normed = low(layer_norm(first_stream, gains[1]))
    hidden = low_back(jnp.dot(normed, up_w, precision=highest))
    acts = low(gelu_tanh(hidden))
    block_out = first_stream + low_back(jnp.dot(acts, down_w, precision=highest))
    second_stream = block_out + attention(block_out, gains[2], qkv_w[1], out_w[1])
    normed_two = layer_norm(second_stream, gains[3])
    logits = jnp.dot(normed_two, router_w, precision=highest)
    one_hot = (expert_index[:, None] == jnp.arange(EXPERTS, dtype=jnp.int32)[None, :]).astype(normed_two.dtype)
    gates = jax.nn.sigmoid(lax.optimization_barrier(jnp.sum(logits * one_hot, axis=-1)))
    rows = low_back(low(normed_two))
    final = second_stream + gates[:, None] * expert_layer(rows, expert_index, e_up, e_down)
    sums = lax.optimization_barrier(jnp.sum(one_hot * gates[:, None], axis=0))
    return (block_out, final, sums)

def to_sequences(array):
    tail = array.shape[1:]
    return jnp.swapaxes(array.reshape((N_DP, N_EXPERT, TOK_DEV) + tail), 0, 1).reshape((SEQS, SEQ_LEN) + tail)

def gather_from_sequences(array):
    tail = array.shape[2:]
    return jnp.swapaxes(array.reshape((N_EXPERT, N_DP, TOK_DEV) + tail), 0, 1).reshape((TOKENS,) + tail)

def reference(tokens, cotangent, expert_ids, loss_weights, section, norm_gains, attn_qkv, attn_out, ffn_up, ffn_down, expert_up, expert_down, router):
    single = jnp.float32
    params = (norm_gains.astype(single), attn_qkv.astype(single), attn_out.astype(single), ffn_up.astype(single), ffn_down.astype(single), expert_up.astype(single), expert_down.astype(single), router.astype(single))
    expert_index = expert_ids[:, 0].astype(jnp.int32)
    counts = lax.optimization_barrier(jnp.sum((expert_index[:, None] == jnp.arange(EXPERTS, dtype=jnp.int32)[None, :]).astype(single), axis=0))
    mean_load = TOKENS / EXPERTS
    coef = (counts - mean_load) / mean_load
    seq_inputs = to_sequences(tokens.astype(single))
    seq_upstream = to_sequences(cotangent.astype(single))
    seq_index = to_sequences(expert_index).astype(jnp.int32)
    seq_weights = loss_weights.astype(single)
    seq_flags = section.astype(single)

    def scan_step(carry_state, item):
        parameter_gradients, totals = carry_state
        inputs, upstream, indices, seq_weight, seq_flag = item
        outputs, pull = jax.vjp(partial(forward, expert_index=indices), params, inputs)
        back_params, back_inputs = pull((jnp.zeros_like(outputs[0]), upstream * seq_weight, seq_flag * (balance_rate / TOKENS) * coef))
        back_params = tuple(back_params[:7]) + (back_params[7] * seq_flag,)
        parameter_gradients = jax.tree.map(jnp.add, parameter_gradients, back_params)
        return ((parameter_gradients, totals + seq_flag * outputs[2]), (outputs[0], outputs[1], back_inputs))
    zero_grads = jax.tree.map(jnp.zeros_like, params)
    (parameter_gradients, totals), (first_block_output, second_block_output, backward_everything) = lax.scan(scan_step, (zero_grads, jnp.zeros((EXPERTS,), single)), (seq_inputs, seq_upstream, seq_index, seq_weights, seq_flags))
    load_balance = jnp.sum(coef * totals) * (balance_rate / TOKENS)
    norm_gains_gradient, query_key_value_gradient, output_projection_gradient, up_projection_gradient, down_projection_gradient, expert_up_gradient, expert_down_gradient, router_weight_gradient = parameter_gradients
    return (gather_from_sequences(first_block_output).astype(jnp.bfloat16), gather_from_sequences(second_block_output).astype(jnp.bfloat16), gather_from_sequences(backward_everything), load_balance, norm_gains_gradient, query_key_value_gradient, output_projection_gradient, up_projection_gradient, down_projection_gradient, expert_up_gradient, expert_down_gradient, router_weight_gradient)
```

```python
import jax
import jax.numpy as jnp
from jax import lax
from jax.experimental import pallas as pl
from jax.experimental.pallas import tpu as pltpu
from jax.sharding import PartitionSpec as P

H = 12
HD = 64


eps_norm = 1e-05
balance_rate = 1.0
bfloat = jnp.bfloat16
single = jnp.float32
highest = lax.Precision.HIGHEST


def norm_forward(stream, gain):
    centre = jnp.mean(stream, axis=-1, keepdims=True)
    centered = stream - centre
    spread = jnp.mean(centered * centered, axis=-1, keepdims=True)
    factor = lax.rsqrt(spread + eps_norm)
    normed = centered * factor
    return (normed * gain, normed, factor)


def norm_backward(upstream, normed, factor, gain):
    grad_normed = upstream * gain
    inner = jnp.mean(grad_normed * normed, axis=-1, keepdims=True)
    centre = jnp.mean(grad_normed, axis=-1, keepdims=True)
    return (factor * (grad_normed - centre - normed * inner), jnp.sum(upstream * normed, axis=0))


def gelu_tanh(hidden):
    return jax.nn.gelu(hidden, approximate=True)


def gelu_back(hidden, upstream):
    return jax.vjp(gelu_tanh, hidden)[1](upstream)[0]


def masked_scores(query_rows, keys, first, offset):
    rows_block = query_rows.shape[0]
    scores = jnp.einsum("qhd,khd->hqk", query_rows, keys, preferred_element_type=single) * HD ** (
        -0.5
    )
    key_place = jnp.arange(keys.shape[0])
    query_place = offset + first + jnp.arange(rows_block)
    allowed = key_place[None, :] <= query_place[:, None]
    return jnp.where(allowed[None], scores, -1e30)


def attend_forward(queries, keys, values, offset):
    row_count = queries.shape[0]
    rows_block = min(512, row_count)

    def one_block(first):
        scores = masked_scores(queries, keys, first, offset)
        largest = jnp.max(scores, axis=-1, keepdims=True)
        weights = jnp.exp(scores - largest)
        weight_sum = jnp.sum(weights, axis=-1, keepdims=True)
        probs = (weights / weight_sum).astype(bfloat)
        mixed = jnp.einsum("hqk,khd->qhd", probs, values, preferred_element_type=single)
        return (mixed.astype(bfloat), (largest + jnp.log(weight_sum))[..., 0])

    starts = jnp.arange(row_count // rows_block, dtype=jnp.int32) * rows_block
    mixed, log_sums = lax.map(one_block, starts)
    return (mixed.reshape(row_count, H * HD), log_sums)


def attend_backward(queries, keys, values, offset, log_sums, grad_mixed):
    row_count = queries.shape[0]
    key_count = keys.shape[0]
    rows_block = min(512, row_count)
    grad_heads = grad_mixed.reshape(row_count, H, HD)

    def one_block(carry_state, item):
        key_grad, value_grad = carry_state
        first, log_block = item
        scores = masked_scores(queries, keys, first, offset)
        probs = jnp.exp(scores - log_block[..., None])
        grad_probs = jnp.einsum("qhd,khd->hqk", grad_heads, values, preferred_element_type=single)
        inner = jnp.sum(probs * grad_probs, axis=-1, keepdims=True)
        grad_scores = (probs * (grad_probs - inner)).astype(bfloat)
        query_grad = jnp.einsum(
            "hqk,khd->qhd", grad_scores, keys, preferred_element_type=single
        ) * HD ** (-0.5)
        key_grad = key_grad + jnp.einsum(
            "hqk,qhd->khd", grad_scores, queries, preferred_element_type=single
        ) * HD ** (-0.5)
        value_grad = value_grad + jnp.einsum(
            "hqk,qhd->khd", probs.astype(bfloat), grad_heads, preferred_element_type=single
        )
        return ((key_grad, value_grad), query_grad)

    starts = jnp.arange(row_count // rows_block, dtype=jnp.int32) * rows_block
    zeros = jnp.zeros((key_count, H, HD), single)
    (key_grad, value_grad), query_grad = lax.scan(one_block, (zeros, zeros), (starts, log_sums))
    return (
        query_grad.reshape(row_count, H * HD),
        key_grad.reshape(key_count, H * HD),
        value_grad.reshape(key_count, H * HD),
    )


def two_chips(stream):
    return lax.axis_size("dp") == 4 and stream.shape[0] % 256 == 0 and stream.shape[1] == H * HD == 768


def attention_forward(stream, gain, w_qkv, w_out, offset):
    if two_chips(stream):
        return attention_forward_fast(stream, gain, w_qkv, w_out)
    row_count, model_width = stream.shape
    normed_out, normed, factor = norm_forward(stream, gain)
    normed_low = normed_out.astype(bfloat)
    packed = jnp.dot(normed_low, w_qkv, preferred_element_type=single).astype(bfloat)
    gathered = lax.all_gather(packed[:, model_width:], "dp", axis=0, tiled=True)
    key_count = gathered.shape[0]
    queries = packed[:, :model_width].reshape(row_count, H, HD)
    keys = gathered[:, :model_width].reshape(key_count, H, HD)
    values = gathered[:, model_width:].reshape(key_count, H, HD)
    mixed, log_sums = attend_forward(queries, keys, values, offset)
    branch = jnp.dot(mixed, w_out, preferred_element_type=single)
    saved = (normed, factor, normed_low, queries, keys, values, log_sums, mixed)
    return (stream + branch, saved)


def attention_backward(upstream, saved, gain, w_qkv, w_out, offset):
    if two_chips(upstream):
        return attention_backward_fast(upstream, saved, gain, w_qkv, w_out)
    normed, factor, normed_low, queries, keys, values, log_sums, mixed = saved
    branch_low = upstream.astype(bfloat)
    out_weight_grad = jnp.dot(mixed.T, branch_low, preferred_element_type=single)
    grad_mixed = jnp.dot(branch_low, w_out.T, preferred_element_type=single).astype(bfloat)
    query_grad, key_grad, value_grad = attend_backward(
        queries, keys, values, offset, log_sums, grad_mixed
    )
    all_grads = jnp.concatenate([key_grad, value_grad], axis=1)
    own_grads = lax.psum_scatter(
        all_grads.astype(jnp.bfloat16), "dp", scatter_dimension=0, tiled=True
    ).astype(jnp.float32)
    packed_grad = jnp.concatenate([query_grad, own_grads], axis=1).astype(bfloat)
    qkv_weight_grad = jnp.dot(normed_low.T, packed_grad, preferred_element_type=single)
    normed_grad = jnp.dot(packed_grad, w_qkv.T, preferred_element_type=single)
    stream_grad, gain_grad = norm_backward(normed_grad, normed, factor, gain)
    return (upstream + stream_grad, gain_grad, qkv_weight_grad, out_weight_grad)


def mm(left, right, dims=((1,), (0,))):
    return lax.dot_general(left, right, (dims, ((), ())), preferred_element_type=single)


NT = ((1,), (1,))
MESH = pl.DeviceIdType.MESH


def head_lanes(shape, head):
    return lax.broadcasted_iota(jnp.int32, shape, 1) // HD == head


def greet(partners):
    barrier = pltpu.get_barrier_semaphore()
    for partner in partners:
        pl.semaphore_signal(barrier, inc=1, device_id=partner, device_id_type=MESH)
    pl.semaphore_wait(barrier, len(partners))


def send(src, dst, send_sem, recv_sem, target):
    return pltpu.make_async_remote_copy(
        src_ref=src,
        dst_ref=dst,
        send_sem=send_sem,
        recv_sem=recv_sem,
        device_id=target,
        device_id_type=MESH,
    )


def pair_forward(q_of, keys, values_t, causal, put, half):
    for j in range(2):
        key_rows = (j + 1) * half if causal else 2 * half
        q = q_of(j) * bfloat(HD**-0.5)
        parts, stats = [], []
        for head in range(2):
            own = jnp.where(head_lanes(q.shape, head), q, bfloat(0))
            scores = mm(keys[:key_rows], own, NT)
            if causal:
                place = lax.broadcasted_iota(jnp.int32, (half, half), 0)
                query = lax.broadcasted_iota(jnp.int32, (half, half), 1)
                last = jnp.where(place <= query, scores[key_rows - half :], -1e30)
                if j:
                    last = jnp.concatenate([scores[: key_rows - half], last], axis=0)
                scores = last
            largest = jnp.max(scores, axis=0, keepdims=True)
            weights = jnp.exp(scores - largest)
            total = jnp.sum(weights, axis=0, keepdims=True)
            mixed = mm(values_t[head * HD : (head + 1) * HD, :key_rows], weights.astype(bfloat))
            parts.append(mixed / total)
            stats.append(largest + jnp.log(total))
        put(j, jnp.transpose(jnp.concatenate(parts, axis=0)).astype(bfloat), stats)


def forward_kernel(
    u_ref, gain_ref, wqkv_ref, wout_ref,
    h_ref, a_ref, o_ref, lse_ref, sv_ref, qx_out_ref,
    own, sv, qx, ox, od, oc, lsx, lsm, lsd, lsc,
    core_sem, q_sem, ox_sem, lsx_sem, od_sem, lsd_sem, local_sem,
):
    place = lax.axis_index("dp")
    ex = lax.axis_index("expert")
    chip = place // 2
    core = lax.rem(place, 2)
    other = 1 - core
    half = u_ref.shape[0]
    width = u_ref.shape[1]
    partner = (chip * 2 + other, ex)
    far = [((1 - chip) * 2 + t, ex) for t in range(2)]
    greet([partner] + far)
    stream = u_ref[...]
    centered = stream - jnp.mean(stream, axis=-1, keepdims=True)
    factor = lax.rsqrt(jnp.mean(centered * centered, axis=-1, keepdims=True) + eps_norm)
    a_ref[...] = (centered * factor * gain_ref[...]).astype(bfloat)
    core_copies = []
    for i in range(3):
        part = mm(a_ref[...], wqkv_ref[:, i * width : (i + 1) * width]).astype(bfloat)
        for p in range(6):
            own[i, p] = part[:, p * 128 : (p + 1) * 128]
        copy = send(
            own.at[i, pl.ds(other * 3, 3)], sv.at[i, :, core], core_sem.at[0, i], core_sem.at[1, i], partner
        )
        copy.start()
        core_copies.append(copy)
        local = pltpu.make_async_copy(own.at[i, pl.ds(core * 3, 3)], sv.at[i, :, core], local_sem.at[i])
        local.start()
        core_copies.append(local)
        if i == 0:

            @pl.when(chip == 1)
            def _():
                for p in range(3):
                    for s in range(2):
                        send(
                            own.at[0, 3 * s + p], qx.at[p, core], q_sem.at[0, p, s], q_sem.at[1, p, core], far[s]
                        ).start()

    for copy in core_copies:
        copy.wait()
    lsm[...] = jnp.zeros_like(lsm)
    lsx[...] = jnp.zeros_like(lsx)

    def diagonal(p):
        keys = sv[1, p].reshape(2 * half, 128)
        values_t = jnp.transpose(sv[2, p].reshape(2 * half, 128).astype(single)).astype(bfloat)

        def put(j, mixed, stats):
            od[j, p] = mixed
            for head in range(2):
                lsm[j, pl.ds(2 * p + head, 1)] = stats[head]

        pair_forward(lambda j: sv[0, p, j], keys, values_t, True, put, half)

    diagonal(0)

    @pl.when(chip == 0)
    def _():
        def cross(p, carry):
            for t in range(2):
                send(own.at[0, 0], qx.at[p, t], q_sem.at[0, p, t], q_sem.at[1, p, t], partner).wait_recv()
            keys = sv[1, p].reshape(2 * half, 128)
            values_t = jnp.transpose(sv[2, p].reshape(2 * half, 128).astype(single)).astype(bfloat)

            def put(j, mixed, stats):
                ox[p, j] = mixed
                for head in range(2):
                    lsx[j, pl.ds(2 * p + head, 1)] = stats[head]

            pair_forward(lambda j: qx[p, j], keys, values_t, False, put, half)
            for t in range(2):
                send(ox.at[p, t], oc.at[core * 3 + p], ox_sem.at[0, p, t], ox_sem.at[1, core * 3 + p, 0], far[t]).start()
            return carry

        lax.fori_loop(0, 3, cross, 0)
        for t in range(2):
            send(lsx.at[t], lsc.at[core], lsx_sem.at[0, t], lsx_sem.at[1, core], far[t]).start()

    for p in range(1, 3):
        diagonal(p)
    back = [
        send(od.at[other], oc.at[pl.ds(6 + core * 3, 3)], od_sem.at[0], od_sem.at[1], partner),
        send(lsm.at[other], lsd, lsd_sem.at[0], lsd_sem.at[1], partner),
    ]
    for copy in back:
        copy.start()
    sv_ref[...] = sv[...]
    for copy in back:
        copy.wait()

    def assemble(s, p):
        mine = s == core
        return jnp.where(mine, od[core, p], oc[6 + s * 3 + p])

    @pl.when(chip == 0)
    def _():
        for s in range(2):
            lse_ref[s] = jnp.where(s == core, lsm[core], lsd[...])
            for p in range(3):
                o_ref[:, (3 * s + p) * 128 : (3 * s + p + 1) * 128] = assemble(s, p)
        qx_out_ref[...] = qx[...]
        for p in range(3):
            for t in range(2):
                send(ox.at[p, t], oc.at[p], ox_sem.at[0, p, t], ox_sem.at[1, p, 0], far[t]).wait_send()
        for t in range(2):
            send(lsx.at[t], lsc.at[t], lsx_sem.at[0, t], lsx_sem.at[1, t], far[t]).wait_send()

    @pl.when(chip == 1)
    def _():
        for p in range(3):
            for s in range(2):
                send(own.at[0, 3 * s + p], qx.at[p, s], q_sem.at[0, p, s], q_sem.at[1, p, s], far[s]).wait_send()
        for s in range(2):
            send(lsx.at[s], lsc.at[s], lsx_sem.at[0, s], lsx_sem.at[1, s], far[s]).wait_recv()
            near = jnp.where(s == core, lsm[core], lsd[...])
            distant = lsc[s]
            top = jnp.maximum(near, distant)
            joint = top + jnp.log(jnp.exp(near - top) + jnp.exp(distant - top))
            lse_ref[s] = joint
            weights = jnp.concatenate([jnp.exp(near - joint), jnp.exp(distant - joint), jnp.zeros((112, half), single)], axis=0)
            weights = jnp.transpose(weights)
            for p in range(3):
                send(ox.at[p, s], oc.at[3 * s + p], ox_sem.at[0, p, s], ox_sem.at[1, 3 * s + p, 0], far[s]).wait_recv()
                lanes = head_lanes((half, 128), 0)
                scale = [jnp.where(lanes, weights[:, r : r + 1], weights[:, r + 1 : r + 2]) for r in (2 * p, 8 + 2 * p)]
                joined = assemble(s, p).astype(single) * scale[0] + oc[3 * s + p].astype(single) * scale[1]
                o_ref[:, (3 * s + p) * 128 : (3 * s + p + 1) * 128] = joined.astype(bfloat)
        qx_out_ref[...] = jnp.zeros_like(qx_out_ref)

    h_ref[...] = u_ref[...] + mm(o_ref[...], wout_ref[...])


def kernel_call(kernel, outs, scratch, collective, flops, vmem=56):
    vmem_spec = pl.BlockSpec(memory_space=pltpu.VMEM)
    return lambda *args: pl.pallas_call(
        kernel,
        out_shape=tuple(jax.ShapeDtypeStruct(*o) for o in outs),
        in_specs=[vmem_spec] * len(args),
        out_specs=tuple(vmem_spec for _ in outs),
        scratch_shapes=scratch,
        compiler_params=pltpu.CompilerParams(
            collective_id=collective, has_side_effects=True, vmem_limit_bytes=vmem * 2**20
        ),
        cost_estimate=pl.CostEstimate(flops=flops, bytes_accessed=12 * 2**20, transcendentals=0),
        name=kernel.__name__,
    )(*args)


def attention_forward_fast(stream, gain, w_qkv, w_out):
    rows, width = stream.shape
    dma, vm = pltpu.SemaphoreType.DMA, pltpu.VMEM
    tile = (rows, 128)
    outs = [
        ((rows, width), single),
        ((rows, width), bfloat),
        ((rows, width), bfloat),
        ((2, 8, rows), single),
        ((3, 3, 2) + tile, bfloat),
        ((3, 2) + tile, bfloat),
    ]
    scratch = [
        vm((3, 6) + tile, bfloat),
        vm((3, 3, 2) + tile, bfloat),
        vm((3, 2) + tile, bfloat),
        vm((3, 2) + tile, bfloat),
        vm((2, 3) + tile, bfloat),
        vm((12,) + tile, bfloat),
        vm((2, 8, rows), single),
        vm((2, 8, rows), single),
        vm((8, rows), single),
        vm((2, 8, rows), single),
        dma((2, 3)),
        dma((2, 3, 2)),
        dma((2, 6, 2)),
        dma((2, 2)),
        dma((2,)),
        dma((2,)),
        dma((3,)),
    ]
    h, a, o, lse, sv, qx = kernel_call(forward_kernel, outs, scratch, 1, 40 * 10**9)(
        stream, gain.reshape(1, width), w_qkv, w_out
    )
    return h, (stream, a, o, lse, sv, qx)


def pair_backward(q_of, do_of, stat_of, keys, keys_t, values, causal, put_query, grads, half):
    key_grad, value_grad, p = grads
    step = half // 2
    for j in range(4):
        key_rows = (j + 1) * step if causal else 2 * half
        q = q_of(j) * bfloat(HD**-0.5)
        do = do_of(j)
        lse, delta = stat_of(j)
        parts = []
        for head in range(2):
            lanes = head_lanes(q.shape, head)
            own_q = jnp.where(lanes, q, bfloat(0))
            own_do = jnp.where(lanes, do, bfloat(0))
            scores = mm(keys[:key_rows], own_q, NT)
            grad_probs = mm(values[:key_rows], own_do, NT)
            probs = jnp.exp(scores - lse[head])
            if causal:
                place = lax.broadcasted_iota(jnp.int32, (step, step), 0)
                query = lax.broadcasted_iota(jnp.int32, (step, step), 1)
                last = jnp.where(place <= query, probs[key_rows - step :], 0.0)
                if j:
                    last = jnp.concatenate([probs[: key_rows - step], last], axis=0)
                probs = last
            grad_scores = (probs * (grad_probs - delta[head])).astype(bfloat)
            value_grad[p, :key_rows] += mm(probs.astype(bfloat), own_do)
            key_grad[p, :key_rows] += mm(grad_scores, own_q)
            parts.append(mm(keys_t[head * HD : (head + 1) * HD, :key_rows], grad_scores))
        put_query(j, jnp.transpose(jnp.concatenate(parts, axis=0)) * HD**-0.5)


def backward_kernel(
    dh_ref, u_ref, gain_ref, o_ref, lse_ref, sv, qx, wqkv_ref, wout_ref,
    du_ref, dgain_ref, dqkv_ref, dbr_ref,
    do_own, st_own, dob, stb, dox, stx, dk, dv, dqs, dkv_out, dqx, dq_far, landed,
    core_sem, st_sem, x_sem, stx_sem, dqx_sem, out_sem, local_sem,
):
    place = lax.axis_index("dp")
    ex = lax.axis_index("expert")
    chip = place // 2
    core = lax.rem(place, 2)
    other = 1 - core
    half, width = u_ref.shape
    partner = (chip * 2 + other, ex)
    far = [((1 - chip) * 2 + t, ex) for t in range(2)]
    greet([partner] + far)
    dbr_ref[...] = dh_ref[...].astype(bfloat)
    do = mm(dbr_ref[...], wout_ref[...], NT).astype(bfloat)
    for p in range(6):
        do_own[p] = do[:, p * 128 : (p + 1) * 128]
    row = lax.broadcasted_iota(jnp.int32, (16, width), 0)
    head_of_row = (row // 8) * 6 + row % 8
    lane_head = lax.broadcasted_iota(jnp.int32, (16, width), 1) // HD
    picks = jnp.where(jnp.logical_and(head_of_row == lane_head, row % 8 < 6), 1.0, 0.0)
    deltas = lax.dot_general(
        picks,
        do.astype(single) * o_ref[...].astype(single),
        (NT, ((), ())),
        precision=highest,
        preferred_element_type=single,
    )
    for s in range(2):
        st_own[s, 0:8] = lse_ref[s]
        st_own[s, 8:16] = deltas[8 * s : 8 * s + 8]
    first = [
        send(st_own.at[other], stb.at[core], st_sem.at[0], st_sem.at[1], partner),
        send(do_own.at[pl.ds(other * 3, 3)], dob.at[:, core], core_sem.at[0], core_sem.at[1], partner),
        pltpu.make_async_copy(st_own.at[core], stb.at[core], local_sem.at[0]),
        pltpu.make_async_copy(do_own.at[pl.ds(core * 3, 3)], dob.at[:, core], local_sem.at[1]),
    ]
    for copy in first:
        copy.start()

    @pl.when(chip == 1)
    def _():
        for s in range(2):
            send(st_own.at[s], stx.at[core], stx_sem.at[0, s], stx_sem.at[1, core], far[s]).start()
        for p in range(3):
            for s in range(2):
                send(do_own.at[3 * s + p], dox.at[p, core], x_sem.at[0, p, s], x_sem.at[1, p, core], far[s]).start()

    dk[...] = jnp.zeros_like(dk)
    dv[...] = jnp.zeros_like(dv)
    for copy in first:
        copy.wait()

    def operands(p):
        keys = sv[1, p].reshape(2 * half, 128)
        keys_t = jnp.transpose(keys.astype(single)).astype(bfloat)
        return keys, keys_t, sv[2, p].reshape(2 * half, 128)

    step = half // 2

    def rows_of(j):
        return pl.ds((j % 2) * step, step)

    def stats_of(ref, p):
        def at(j):
            cols = slice((j % 2) * step, (j % 2 + 1) * step)
            lse = [ref[j // 2, pl.ds(2 * p + head, 1), cols] for head in range(2)]
            delta = [ref[j // 2, pl.ds(8 + 2 * p + head, 1), cols] for head in range(2)]
            return lse, delta

        return at

    def diagonal(p):
        keys, keys_t, values = operands(p)

        def put(j, grad):
            dqs[p, j // 2, rows_of(j)] = grad.astype(bfloat)

        pair_backward(
            lambda j: sv[0, p, j // 2, rows_of(j)],
            lambda j: dob[p, j // 2, rows_of(j)],
            stats_of(stb, p), keys, keys_t, values, True, put, (dk, dv, p), half,
        )

    diagonal(0)

    @pl.when(chip == 0)
    def _():
        for t in range(2):
            send(st_own.at[0], stx.at[t], stx_sem.at[0, t], stx_sem.at[1, t], partner).wait_recv()

        def cross(p, carry):
            for t in range(2):
                send(do_own.at[0], dox.at[p, t], x_sem.at[0, p, t], x_sem.at[1, p, t], partner).wait_recv()
            keys, keys_t, values = operands(p)

            def put(j, grad):
                dqx[p, j // 2, rows_of(j)] = grad.astype(bfloat)

            pair_backward(
                lambda j: qx[p, j // 2, rows_of(j)],
                lambda j: dox[p, j // 2, rows_of(j)],
                stats_of(stx, p), keys, keys_t, values, False, put, (dk, dv, p), half,
            )
            for t in range(2):
                send(dqx.at[p, t], dq_far.at[core * 3 + p], dqx_sem.at[0, p, t], dqx_sem.at[1, core * 3 + p, 0], far[t]).start()
            return carry

        lax.fori_loop(0, 3, cross, 0)

    for p in range(1, 3):
        diagonal(p)
    for p in range(3):
        for t in range(2):
            rows = slice(t * half, (t + 1) * half)
            dkv_out[t, 0, p] = dqs[p, t]
            dkv_out[t, 1, p] = dk[p, rows].astype(bfloat)
            dkv_out[t, 2, p] = dv[p, rows].astype(bfloat)
    last = send(dkv_out.at[other], landed, out_sem.at[0], out_sem.at[1], partner)
    last.start()
    last.wait()

    for i in range(3):
        for s in range(2):
            for p in range(3):
                part = jnp.where(s == core, dkv_out[core, i, p], landed[i, p])
                dqkv_ref[:, i * width + (3 * s + p) * 128 : i * width + (3 * s + p + 1) * 128] = part

    @pl.when(chip == 0)
    def _():
        for p in range(3):
            for t in range(2):
                send(dqx.at[p, t], dq_far.at[p], dqx_sem.at[0, p, t], dqx_sem.at[1, p, 0], far[t]).wait_send()

    @pl.when(chip == 1)
    def _():
        for s in range(2):
            send(st_own.at[s], stx.at[s], stx_sem.at[0, s], stx_sem.at[1, s], far[s]).wait_send()
        for p in range(3):
            for s in range(2):
                send(do_own.at[3 * s + p], dox.at[p, s], x_sem.at[0, p, s], x_sem.at[1, p, s], far[s]).wait_send()
        for s in range(2):
            for p in range(3):
                q = 3 * s + p
                send(dqx.at[p, s], dq_far.at[q], dqx_sem.at[0, p, s], dqx_sem.at[1, q, 0], far[s]).wait_recv()
                cols = slice(q * 128, (q + 1) * 128)
                dqkv_ref[:, cols] = (dqkv_ref[:, cols].astype(single) + dq_far[q].astype(single)).astype(bfloat)

    da = mm(dqkv_ref[...], wqkv_ref[...], NT)
    stream = u_ref[...]
    centered = stream - jnp.mean(stream, axis=-1, keepdims=True)
    factor = lax.rsqrt(jnp.mean(centered * centered, axis=-1, keepdims=True) + eps_norm)
    normed = centered * factor
    dgain_ref[...] = jnp.sum(da * normed, axis=0, keepdims=True)
    dn = da * gain_ref[...]
    inner = jnp.mean(dn * normed, axis=-1, keepdims=True)
    du_ref[...] = dh_ref[...] + factor * (dn - jnp.mean(dn, axis=-1, keepdims=True) - normed * inner)


def attention_backward_fast(upstream, saved, gain, w_qkv, w_out):
    stream, a, o, lse, sv, qx = saved
    rows, width = stream.shape
    dma, vm = pltpu.SemaphoreType.DMA, pltpu.VMEM
    tile = (rows, 128)
    outs = [((rows, width), single), ((1, width), single), ((rows, 3 * width), bfloat), ((rows, width), bfloat)]
    scratch = [
        vm((6,) + tile, bfloat),
        vm((2, 16, rows), single),
        vm((3, 2) + tile, bfloat),
        vm((2, 16, rows), single),
        vm((3, 2) + tile, bfloat),
        vm((2, 16, rows), single),
        vm((3, 2 * rows, 128), single),
        vm((3, 2 * rows, 128), single),
        vm((3, 2) + tile, bfloat),
        vm((2, 3, 3) + tile, bfloat),
        vm((3, 2) + tile, bfloat),
        vm((6,) + tile, bfloat),
        vm((3, 3) + tile, bfloat),
        dma((2,)),
        dma((2,)),
        dma((2, 3, 2)),
        dma((2, 2)),
        dma((2, 6, 2)),
        dma((2,)),
        dma((2,)),
    ]
    du, dgain, dqkv, dbr = kernel_call(backward_kernel, outs, scratch, 2, 60 * 10**9)(
        upstream, stream, gain.reshape(1, width), o, lse, sv, qx, w_qkv, w_out
    )
    out_weight_grad = jnp.dot(o.T, dbr, preferred_element_type=single)
    qkv_weight_grad = jnp.dot(a.T, dqkv, preferred_element_type=single)
    return du, dgain[0], qkv_weight_grad, out_weight_grad


def routing(expert_ids, expert_count, capacity):
    indices = expert_ids[:, 0]
    one_hot = (indices[:, None] == jnp.arange(expert_count, dtype=jnp.int32)[None, :]).astype(
        jnp.int32
    )
    earlier = jnp.cumsum(one_hot, axis=0) - one_hot
    slots = jnp.sum(earlier * one_hot, axis=1)
    kept_rows = slots < capacity
    target = jnp.where(kept_rows, indices * capacity + slots, expert_count * capacity)
    return (one_hot.astype(single), target, kept_rows)


def body(
    tokens,
    cotangent,
    expert_ids,
    loss_weights,
    section,
    norm_gains,
    attn_qkv,
    attn_out,
    ffn_up,
    ffn_down,
    expert_up,
    expert_down,
    router,
):
    row_count, model_width = tokens.shape
    expert_count = router.shape[1]
    capacity = 5 * row_count // (4 * expert_count)
    slots_all = expert_count * capacity
    group_count = lax.axis_size("expert")
    total_tokens = row_count * lax.axis_size("dp") * group_count
    offset = lax.axis_index("dp") * row_count
    sequence = lax.axis_index("expert")
    switch = section[sequence].astype(single)
    seq_weight = loss_weights[sequence].astype(single)
    inputs = tokens.astype(single)
    first_stream, saved_one = attention_forward(
        inputs, norm_gains[0], attn_qkv[0], attn_out[0], offset
    )
    ffn_out, ffn_normed, ffn_factor = norm_forward(first_stream, norm_gains[1])
    ffn_low = ffn_out.astype(bfloat)
    hidden = jnp.dot(ffn_low, ffn_up, preferred_element_type=single)
    acts_low = gelu_tanh(hidden).astype(bfloat)
    block_out = first_stream + jnp.dot(acts_low, ffn_down, preferred_element_type=single)
    second_stream, saved_two = attention_forward(
        block_out, norm_gains[2], attn_qkv[1], attn_out[1], offset
    )
    moe_in, moe_normed, moe_factor = norm_forward(second_stream, norm_gains[3])
    logits = jnp.dot(moe_in, router, precision=highest)
    one_hot, target, kept_rows = routing(expert_ids, expert_count, capacity)
    gates = jax.nn.sigmoid(jnp.sum(logits * one_hot, axis=1))
    outgoing = (
        jnp.zeros((slots_all, model_width), bfloat)
        .at[target]
        .set(moe_in.astype(bfloat), mode="drop")
    )
    arrived = lax.all_to_all(
        outgoing.reshape(expert_count, capacity, model_width),
        "expert",
        split_axis=0,
        concat_axis=0,
        tiled=True,
    )
    expert_rows = arrived.reshape(-1, model_width)
    expert_hidden = jnp.dot(expert_rows, expert_up[0], preferred_element_type=single)
    expert_acts = gelu_tanh(expert_hidden).astype(bfloat)
    expert_result = jnp.dot(expert_acts, expert_down[0], preferred_element_type=single).astype(
        bfloat
    )
    returned = lax.all_to_all(
        expert_result.reshape(group_count, capacity, model_width),
        "expert",
        split_axis=0,
        concat_axis=0,
        tiled=True,
    )
    safe_target = jnp.minimum(target, slots_all - 1)
    kept_float = kept_rows.astype(single)[:, None]
    moe_out = returned.reshape(slots_all, model_width)[safe_target].astype(single) * kept_float
    final = second_stream + gates[:, None] * moe_out
    counts, gate_sums = lax.psum(
        (jnp.sum(one_hot, axis=0), switch * jnp.sum(one_hot * gates[:, None], axis=0)),
        ("dp", "expert"),
    )
    mean_load = total_tokens / expert_count
    coef = (counts - mean_load) / mean_load
    load_balance = jnp.sum(coef * gate_sums) * (balance_rate / total_tokens)
    final_grad = cotangent.astype(single) * seq_weight
    gate_slope = gates * (1.0 - gates)
    gate_grad = jnp.sum(final_grad * moe_out, axis=1)
    balance_term = switch * (balance_rate / total_tokens) * jnp.sum(one_hot * coef[None, :], axis=1)
    logit_grad = (gate_grad + balance_term) * gate_slope
    result_grad = (final_grad * gates[:, None]).astype(bfloat)
    outgoing_grad = (
        jnp.zeros((slots_all, model_width), bfloat).at[target].set(result_grad, mode="drop")
    )
    grad_rows = lax.all_to_all(
        outgoing_grad.reshape(expert_count, capacity, model_width),
        "expert",
        split_axis=0,
        concat_axis=0,
        tiled=True,
    ).reshape(-1, model_width)
    down_expert_grad = jnp.dot(expert_acts.T, grad_rows, preferred_element_type=single)
    grad_acts = jnp.dot(grad_rows, expert_down[0].T, preferred_element_type=single)
    grad_hidden = gelu_back(expert_hidden, grad_acts).astype(bfloat)
    up_expert_grad = jnp.dot(expert_rows.T, grad_hidden, preferred_element_type=single)
    grad_inputs = jnp.dot(grad_hidden, expert_up[0].T, preferred_element_type=single).astype(bfloat)
    grad_back = lax.all_to_all(
        grad_inputs.reshape(group_count, capacity, model_width),
        "expert",
        split_axis=0,
        concat_axis=0,
        tiled=True,
    )
    moe_in_grad = grad_back.reshape(slots_all, model_width)[safe_target].astype(single) * kept_float
    routed_grad = logit_grad[:, None] * one_hot
    moe_in_grad = moe_in_grad + jnp.dot(routed_grad, router.T, precision=highest)
    router_local = switch * jnp.dot(moe_in.T, routed_grad, precision=highest)
    norm_grad_two, gain_three = norm_backward(moe_in_grad, moe_normed, moe_factor, norm_gains[3])
    second_grad = final_grad + norm_grad_two
    block_grad, gain_two, qkv_two, out_two = attention_backward(
        second_grad, saved_two, norm_gains[2], attn_qkv[1], attn_out[1], offset
    )
    branch_low = block_grad.astype(bfloat)
    down_local = jnp.dot(acts_low.T, branch_low, preferred_element_type=single)
    grad_dense_acts = jnp.dot(branch_low, ffn_down.T, preferred_element_type=single)
    grad_dense_hidden = gelu_back(hidden, grad_dense_acts).astype(bfloat)
    up_local = jnp.dot(ffn_low.T, grad_dense_hidden, preferred_element_type=single)
    ffn_in_grad = jnp.dot(grad_dense_hidden, ffn_up.T, preferred_element_type=single)
    norm_grad_one, gain_one = norm_backward(ffn_in_grad, ffn_normed, ffn_factor, norm_gains[1])
    first_grad = block_grad + norm_grad_one
    input_grad, gain_zero, qkv_one, out_one = attention_backward(
        first_grad, saved_one, norm_gains[0], attn_qkv[0], attn_out[0], offset
    )
    expert_up_part, expert_down_part = (
        lax.psum_scatter(
            up_expert_grad[None].astype(jnp.bfloat16), "dp", scatter_dimension=1, tiled=True
        ).astype(jnp.float32),
        lax.psum_scatter(
            down_expert_grad[None].astype(jnp.bfloat16), "dp", scatter_dimension=1, tiled=True
        ).astype(jnp.float32),
    )
    gains_local = jnp.stack([gain_zero, gain_one, gain_two, gain_three])
    gains_total, router_total = lax.psum((gains_local, router_local), ("dp", "expert"))
    qkv_local = jnp.stack([qkv_one, qkv_two])
    out_local = jnp.stack([out_one, out_two])
    qkv_part, out_part, up_part, down_part = (
        lax.psum_scatter(
            qkv_local.astype(jnp.bfloat16), "expert", scatter_dimension=1, tiled=True
        ).astype(jnp.float32),
        lax.psum_scatter(
            out_local.astype(jnp.bfloat16), "expert", scatter_dimension=1, tiled=True
        ).astype(jnp.float32),
        lax.psum_scatter(
            up_local.astype(jnp.bfloat16), "expert", scatter_dimension=0, tiled=True
        ).astype(jnp.float32),
        lax.psum_scatter(
            down_local.astype(jnp.bfloat16), "expert", scatter_dimension=0, tiled=True
        ).astype(jnp.float32),
    )
    qkv_part, out_part, up_part, down_part = (
        lax.psum(qkv_part.astype(jnp.bfloat16), "dp").astype(jnp.float32),
        lax.psum(out_part.astype(jnp.bfloat16), "dp").astype(jnp.float32),
        lax.psum(up_part.astype(jnp.bfloat16), "dp").astype(jnp.float32),
        lax.psum(down_part.astype(jnp.bfloat16), "dp").astype(jnp.float32),
    )
    return (
        block_out.astype(bfloat),
        final.astype(bfloat),
        input_grad,
        load_balance,
        gains_total,
        qkv_part,
        out_part,
        up_part,
        down_part,
        expert_up_part,
        expert_down_part,
        router_total,
    )


def solution(mesh):
    in_specs = (
        P(("dp", "expert"), None),
        P(("dp", "expert"), None),
        P(("dp", "expert"), None),
        P(),
        P(),
        P(),
        P(),
        P(),
        P(),
        P(),
        P("expert", None, None),
        P("expert", None, None),
        P(),
    )
    out_specs = (
        P(("dp", "expert"), None),
        P(("dp", "expert"), None),
        P(("dp", "expert"), None),
        P(),
        P(),
        P(None, "expert", None),
        P(None, "expert", None),
        P("expert", None),
        P("expert", None),
        P("expert", "dp", None),
        P("expert", "dp", None),
        P(),
    )
    return jax.shard_map(body, mesh=mesh, in_specs=in_specs, out_specs=out_specs, check_vma=False)
```

```python
import functools

import jax
import jax.numpy as jnp
from jax import lax
from jax.experimental import pallas as pl
from jax.experimental.pallas import tpu as pltpu
from jax.sharding import PartitionSpec as P

H = 12
HD = 64


eps_norm = 1e-05
balance_rate = 1.0
bfloat = jnp.bfloat16
single = jnp.float32
highest = lax.Precision.HIGHEST


def norm_forward(stream, gain):
    centre = jnp.mean(stream, axis=-1, keepdims=True)
    centered = stream - centre
    spread = jnp.mean(centered * centered, axis=-1, keepdims=True)
    factor = lax.rsqrt(spread + eps_norm)
    normed = centered * factor
    return (normed * gain, normed, factor)


def norm_backward(upstream, normed, factor, gain):
    grad_normed = upstream * gain
    inner = jnp.mean(grad_normed * normed, axis=-1, keepdims=True)
    centre = jnp.mean(grad_normed, axis=-1, keepdims=True)
    return (factor * (grad_normed - centre - normed * inner), jnp.sum(upstream * normed, axis=0))


def gelu_tanh(hidden):
    return jax.nn.gelu(hidden, approximate=True)


def gelu_back(hidden, upstream):
    return jax.vjp(gelu_tanh, hidden)[1](upstream)[0]


def masked_scores(query_rows, keys, first, offset):
    rows_block = query_rows.shape[0]
    scores = jnp.einsum("qhd,khd->hqk", query_rows, keys, preferred_element_type=single) * HD ** (
        -0.5
    )
    key_place = jnp.arange(keys.shape[0])
    query_place = offset + first + jnp.arange(rows_block)
    allowed = key_place[None, :] <= query_place[:, None]
    return jnp.where(allowed[None], scores, -1e30)


def attend_forward(queries, keys, values, offset):
    row_count = queries.shape[0]
    rows_block = min(512, row_count)

    def one_block(first):
        scores = masked_scores(queries, keys, first, offset)
        largest = jnp.max(scores, axis=-1, keepdims=True)
        weights = jnp.exp(scores - largest)
        weight_sum = jnp.sum(weights, axis=-1, keepdims=True)
        probs = (weights / weight_sum).astype(bfloat)
        mixed = jnp.einsum("hqk,khd->qhd", probs, values, preferred_element_type=single)
        return (mixed.astype(bfloat), (largest + jnp.log(weight_sum))[..., 0])

    starts = jnp.arange(row_count // rows_block, dtype=jnp.int32) * rows_block
    mixed, log_sums = lax.map(one_block, starts)
    return (mixed.reshape(row_count, H * HD), log_sums)


def attend_backward(queries, keys, values, offset, log_sums, grad_mixed):
    row_count = queries.shape[0]
    key_count = keys.shape[0]
    rows_block = min(512, row_count)
    grad_heads = grad_mixed.reshape(row_count, H, HD)

    def one_block(carry_state, item):
        key_grad, value_grad = carry_state
        first, log_block = item
        scores = masked_scores(queries, keys, first, offset)
        probs = jnp.exp(scores - log_block[..., None])
        grad_probs = jnp.einsum("qhd,khd->hqk", grad_heads, values, preferred_element_type=single)
        inner = jnp.sum(probs * grad_probs, axis=-1, keepdims=True)
        grad_scores = (probs * (grad_probs - inner)).astype(bfloat)
        query_grad = jnp.einsum(
            "hqk,khd->qhd", grad_scores, keys, preferred_element_type=single
        ) * HD ** (-0.5)
        key_grad = key_grad + jnp.einsum(
            "hqk,qhd->khd", grad_scores, queries, preferred_element_type=single
        ) * HD ** (-0.5)
        value_grad = value_grad + jnp.einsum(
            "hqk,qhd->khd", probs.astype(bfloat), grad_heads, preferred_element_type=single
        )
        return ((key_grad, value_grad), query_grad)

    starts = jnp.arange(row_count // rows_block, dtype=jnp.int32) * rows_block
    zeros = jnp.zeros((key_count, H, HD), single)
    (key_grad, value_grad), query_grad = lax.scan(one_block, (zeros, zeros), (starts, log_sums))
    return (
        query_grad.reshape(row_count, H * HD),
        key_grad.reshape(key_count, H * HD),
        value_grad.reshape(key_count, H * HD),
    )


def attention_forward(stream, gain, w_qkv, w_out, offset):
    row_count, model_width = stream.shape
    normed_out, normed, factor = norm_forward(stream, gain)
    normed_low = normed_out.astype(bfloat)
    packed = jnp.dot(normed_low, w_qkv, preferred_element_type=single).astype(bfloat)
    gathered = lax.all_gather(packed[:, model_width:], "dp", axis=0, tiled=True)
    key_count = gathered.shape[0]
    queries = packed[:, :model_width].reshape(row_count, H, HD)
    keys = gathered[:, :model_width].reshape(key_count, H, HD)
    values = gathered[:, model_width:].reshape(key_count, H, HD)
    mixed, log_sums = attend_forward(queries, keys, values, offset)
    branch = jnp.dot(mixed, w_out, preferred_element_type=single)
    saved = (normed, factor, normed_low, queries, keys, values, log_sums, mixed)
    return (stream + branch, saved)


def attention_backward(upstream, saved, gain, w_qkv, w_out, offset):
    normed, factor, normed_low, queries, keys, values, log_sums, mixed = saved
    branch_low = upstream.astype(bfloat)
    out_weight_grad = jnp.dot(mixed.T, branch_low, preferred_element_type=single)
    grad_mixed = jnp.dot(branch_low, w_out.T, preferred_element_type=single).astype(bfloat)
    query_grad, key_grad, value_grad = attend_backward(
        queries, keys, values, offset, log_sums, grad_mixed
    )
    all_grads = jnp.concatenate([key_grad, value_grad], axis=1)
    own_grads = lax.psum_scatter(
        all_grads.astype(jnp.bfloat16), "dp", scatter_dimension=0, tiled=True
    ).astype(jnp.float32)
    packed_grad = jnp.concatenate([query_grad, own_grads], axis=1).astype(bfloat)
    qkv_weight_grad = jnp.dot(normed_low.T, packed_grad, preferred_element_type=single)
    normed_grad = jnp.dot(packed_grad, w_qkv.T, preferred_element_type=single)
    stream_grad, gain_grad = norm_backward(normed_grad, normed, factor, gain)
    return (upstream + stream_grad, gain_grad, qkv_weight_grad, out_weight_grad)


def mm(left, right, dims=((1,), (0,))):
    return lax.dot_general(left, right, (dims, ((), ())), preferred_element_type=single)


NT = ((1,), (1,))
MESH = pl.DeviceIdType.MESH


def head_lanes(shape, head):
    return lax.broadcasted_iota(jnp.int32, shape, 1) // HD == head


def greet(partners):
    barrier = pltpu.get_barrier_semaphore()
    for partner in partners:
        pl.semaphore_signal(barrier, inc=1, device_id=partner, device_id_type=MESH)
    pl.semaphore_wait(barrier, len(partners))


def send(src, dst, send_sem, recv_sem, target):
    return pltpu.make_async_remote_copy(
        src_ref=src,
        dst_ref=dst,
        send_sem=send_sem,
        recv_sem=recv_sem,
        device_id=target,
        device_id_type=MESH,
    )


def pair_forward(q_of, keys, values_t, causal, put, half):
    for j in range(2):
        key_rows = (j + 1) * half if causal else 2 * half
        q = q_of(j) * bfloat(HD**-0.5)
        parts, stats = [], []
        for head in range(2):
            own = jnp.where(head_lanes(q.shape, head), q, bfloat(0))
            scores = mm(keys[:key_rows], own, NT)
            if causal:
                place = lax.broadcasted_iota(jnp.int32, (half, half), 0)
                query = lax.broadcasted_iota(jnp.int32, (half, half), 1)
                last = jnp.where(place <= query, scores[key_rows - half :], -1e30)
                if j:
                    last = jnp.concatenate([scores[: key_rows - half], last], axis=0)
                scores = last
            largest = jnp.max(scores, axis=0, keepdims=True)
            weights = jnp.exp(scores - largest)
            total = jnp.sum(weights, axis=0, keepdims=True)
            mixed = mm(values_t[head * HD : (head + 1) * HD, :key_rows], weights.astype(bfloat))
            parts.append(mixed / total)
            stats.append(largest + jnp.log(total))
        put(j, jnp.transpose(jnp.concatenate(parts, axis=0)).astype(bfloat), stats)


def forward_kernel(
    index, u_ref, gain_ref, wqkv_any, wout_any, count_ref,
    h_ref, a_ref, o_ref, lse_ref, sv_ref, qx_out_ref, counts_ref,
    own, sv, qx, ox, od, oc, lsx, lsm, lsd, lsc,
    core_sem, q_sem, ox_sem, lsx_sem, od_sem, lsd_sem, local_sem, wqkv_ref, wout_ref, w_sem, counts_in, count_sem,
):
    place = lax.axis_index("dp")
    ex = lax.axis_index("expert")
    chip = place // 2
    core = lax.rem(place, 2)
    other = 1 - core
    half = u_ref.shape[0]
    width = u_ref.shape[1]
    partner = (chip * 2 + other, ex)
    far = [((1 - chip) * 2 + t, ex) for t in range(2)]
    loads = [
        pltpu.make_async_copy(
            wqkv_any.at[index, :, pl.ds(i * width, width)], wqkv_ref.at[:, pl.ds(i * width, width)], w_sem.at[i]
        )
        for i in range(3)
    ]
    loads.append(pltpu.make_async_copy(wout_any.at[index], wout_ref, w_sem.at[3]))
    for load in loads:
        load.start()
    greet([partner] + far)
    count_copies = [
        send(count_ref, counts_in.at[i], count_sem.at[0, i], count_sem.at[1, i], to)
        for i, to in enumerate([partner, (lax.rem(place + 2, 4), ex), (3 - place, ex)])
    ]
    for copy in count_copies:
        copy.start()
    stream = u_ref[...]
    centered = stream - jnp.mean(stream, axis=-1, keepdims=True)
    factor = lax.rsqrt(jnp.mean(centered * centered, axis=-1, keepdims=True) + eps_norm)
    a_ref[...] = (centered * factor * gain_ref[2 * index : 2 * index + 1]).astype(bfloat)
    core_copies = []
    for i in range(3):
        loads[i].wait()
        part = mm(a_ref[...], wqkv_ref[:, i * width : (i + 1) * width]).astype(bfloat)
        for p in range(6):
            own[i, p] = part[:, p * 128 : (p + 1) * 128]
        copy = send(
            own.at[i, pl.ds(other * 3, 3)], sv.at[i, :, core], core_sem.at[0, i], core_sem.at[1, i], partner
        )
        copy.start()
        core_copies.append(copy)
        local = pltpu.make_async_copy(own.at[i, pl.ds(core * 3, 3)], sv.at[i, :, core], local_sem.at[i])
        local.start()
        core_copies.append(local)
        if i == 0:

            @pl.when(chip == 1)
            def _():
                for p in range(3):
                    for s in range(2):
                        send(
                            own.at[0, 3 * s + p], qx.at[p, core], q_sem.at[0, p, s], q_sem.at[1, p, core], far[s]
                        ).start()

    for copy in core_copies:
        copy.wait()
    lsm[...] = jnp.zeros_like(lsm)
    lsx[...] = jnp.zeros_like(lsx)

    def diagonal(p):
        keys = sv[1, p].reshape(2 * half, 128)
        values_t = jnp.transpose(sv[2, p].reshape(2 * half, 128).astype(single)).astype(bfloat)

        def put(j, mixed, stats):
            od[j, p] = mixed
            for head in range(2):
                lsm[j, pl.ds(2 * p + head, 1)] = stats[head]

        pair_forward(lambda j: sv[0, p, j], keys, values_t, True, put, half)

    diagonal(0)

    @pl.when(chip == 0)
    def _():
        def cross(p, carry):
            for t in range(2):
                send(own.at[0, 0], qx.at[p, t], q_sem.at[0, p, t], q_sem.at[1, p, t], partner).wait_recv()
            keys = sv[1, p].reshape(2 * half, 128)
            values_t = jnp.transpose(sv[2, p].reshape(2 * half, 128).astype(single)).astype(bfloat)

            def put(j, mixed, stats):
                ox[p, j] = mixed
                for head in range(2):
                    lsx[j, pl.ds(2 * p + head, 1)] = stats[head]

            pair_forward(lambda j: qx[p, j], keys, values_t, False, put, half)
            for t in range(2):
                send(ox.at[p, t], oc.at[core * 3 + p], ox_sem.at[0, p, t], ox_sem.at[1, core * 3 + p, 0], far[t]).start()
            return carry

        lax.fori_loop(0, 3, cross, 0)
        for t in range(2):
            send(lsx.at[t], lsc.at[core], lsx_sem.at[0, t], lsx_sem.at[1, core], far[t]).start()

    for p in range(1, 3):
        diagonal(p)
    back = [
        send(od.at[other], oc.at[pl.ds(6 + core * 3, 3)], od_sem.at[0], od_sem.at[1], partner),
        send(lsm.at[other], lsd, lsd_sem.at[0], lsd_sem.at[1], partner),
    ]
    for copy in back:
        copy.start()
    sv_ref[...] = sv[...]
    for copy in back:
        copy.wait()

    def assemble(s, p):
        mine = s == core
        return jnp.where(mine, od[core, p], oc[6 + s * 3 + p])

    @pl.when(chip == 0)
    def _():
        for s in range(2):
            lse_ref[s] = jnp.where(s == core, lsm[core], lsd[...])
            for p in range(3):
                o_ref[:, (3 * s + p) * 128 : (3 * s + p + 1) * 128] = assemble(s, p)
        qx_out_ref[...] = qx[...]
        for p in range(3):
            for t in range(2):
                send(ox.at[p, t], oc.at[p], ox_sem.at[0, p, t], ox_sem.at[1, p, 0], far[t]).wait_send()
        for t in range(2):
            send(lsx.at[t], lsc.at[t], lsx_sem.at[0, t], lsx_sem.at[1, t], far[t]).wait_send()

    @pl.when(chip == 1)
    def _():
        for p in range(3):
            for s in range(2):
                send(own.at[0, 3 * s + p], qx.at[p, s], q_sem.at[0, p, s], q_sem.at[1, p, s], far[s]).wait_send()
        for s in range(2):
            send(lsx.at[s], lsc.at[s], lsx_sem.at[0, s], lsx_sem.at[1, s], far[s]).wait_recv()
            near = jnp.where(s == core, lsm[core], lsd[...])
            distant = lsc[s]
            top = jnp.maximum(near, distant)
            joint = top + jnp.log(jnp.exp(near - top) + jnp.exp(distant - top))
            lse_ref[s] = joint
            weights = jnp.concatenate([jnp.exp(near - joint), jnp.exp(distant - joint), jnp.zeros((112, half), single)], axis=0)
            weights = jnp.transpose(weights)
            for p in range(3):
                send(ox.at[p, s], oc.at[3 * s + p], ox_sem.at[0, p, s], ox_sem.at[1, 3 * s + p, 0], far[s]).wait_recv()
                lanes = head_lanes((half, 128), 0)
                scale = [jnp.where(lanes, weights[:, r : r + 1], weights[:, r + 1 : r + 2]) for r in (2 * p, 8 + 2 * p)]
                joined = assemble(s, p).astype(single) * scale[0] + oc[3 * s + p].astype(single) * scale[1]
                o_ref[:, (3 * s + p) * 128 : (3 * s + p + 1) * 128] = joined.astype(bfloat)
        qx_out_ref[...] = jnp.zeros_like(qx_out_ref)

    loads[3].wait()
    for copy in count_copies:
        copy.wait()
    counts_ref[...] = count_ref[...] + counts_in[0] + counts_in[1] + counts_in[2]
    h_ref[...] = u_ref[...] + mm(o_ref[...], wout_ref[...])


names = (
    "forward_zero", "forward_one", "backward_zero", "backward_one", "attention_weights_one", "attention_weights_two",
    "ffn_up_weights", "ffn_down_weights", "experts",
)


def kernel_call(kernel, outs, scratch, name, flops, stay=(), vmem=56):
    vmem_spec = pl.BlockSpec(memory_space=pltpu.VMEM)
    return lambda *args: pl.pallas_call(
        kernel,
        out_shape=tuple(jax.ShapeDtypeStruct(*o) for o in outs),
        in_specs=[pl.BlockSpec(memory_space=pl.ANY) if i in stay else vmem_spec for i in range(len(args))],
        out_specs=tuple(vmem_spec for _ in outs),
        scratch_shapes=scratch,
        compiler_params=pltpu.CompilerParams(
            collective_id=1 + names.index(name), has_side_effects=True, vmem_limit_bytes=vmem * 2**20
        ),
        cost_estimate=pl.CostEstimate(flops=flops, bytes_accessed=12 * 2**20, transcendentals=0),
        name=name,
    )(*args)


def attention_forward_fast(stream, gains, w_qkv, w_out, counts, index):
    rows, width = stream.shape
    dma, vm = pltpu.SemaphoreType.DMA, pltpu.VMEM
    tile = (rows, 128)
    outs = [
        ((rows, width), single),
        ((rows, width), bfloat),
        ((rows, width), bfloat),
        ((2, 8, rows), single),
        ((3, 3, 2) + tile, bfloat),
        ((3, 2) + tile, bfloat),
        ((8, 128), single),
    ]
    scratch = [
        vm((3, 6) + tile, bfloat),
        vm((3, 3, 2) + tile, bfloat),
        vm((3, 2) + tile, bfloat),
        vm((3, 2) + tile, bfloat),
        vm((2, 3) + tile, bfloat),
        vm((12,) + tile, bfloat),
        vm((2, 8, rows), single),
        vm((2, 8, rows), single),
        vm((8, rows), single),
        vm((2, 8, rows), single),
        dma((2, 3)),
        dma((2, 3, 2)),
        dma((2, 6, 2)),
        dma((2, 2)),
        dma((2,)),
        dma((2,)),
        dma((3,)),
        vm(w_qkv.shape[1:], bfloat),
        vm(w_out.shape[1:], bfloat),
        dma((4,)),
        vm((3, 8, 128), single),
        dma((2, 3)),
    ]
    h, a, o, lse, sv, qx, counts = kernel_call(
        functools.partial(forward_kernel, index),
        outs,
        scratch,
        ("forward_zero", "forward_one")[index],
        40 * 10**9,
        (2, 3),
    )(stream, gains, w_qkv, w_out, counts)
    return h, (stream, a, o, lse, sv, qx), counts


def pair_backward(q_of, do_of, stat_of, keys, keys_t, values, causal, put_query, grads, half):
    key_grad, value_grad, p = grads
    step = half // 2
    for j in range(4):
        key_rows = (j + 1) * step if causal else 2 * half
        q = q_of(j) * bfloat(HD**-0.5)
        do = do_of(j)
        lse, delta = stat_of(j)
        parts = []
        for head in range(2):
            lanes = head_lanes(q.shape, head)
            own_q = jnp.where(lanes, q, bfloat(0))
            own_do = jnp.where(lanes, do, bfloat(0))
            scores = mm(keys[:key_rows], own_q, NT)
            grad_probs = mm(values[:key_rows], own_do, NT)
            probs = jnp.exp(scores - lse[head])
            if causal:
                place = lax.broadcasted_iota(jnp.int32, (step, step), 0)
                query = lax.broadcasted_iota(jnp.int32, (step, step), 1)
                last = jnp.where(place <= query, probs[key_rows - step :], 0.0)
                if j:
                    last = jnp.concatenate([probs[: key_rows - step], last], axis=0)
                probs = last
            grad_scores = (probs * (grad_probs - delta[head])).astype(bfloat)
            value_grad[p, :key_rows] += mm(probs.astype(bfloat), own_do)
            key_grad[p, :key_rows] += mm(grad_scores, own_q)
            parts.append(mm(keys_t[head * HD : (head + 1) * HD, :key_rows], grad_scores))
        put_query(j, jnp.transpose(jnp.concatenate(parts, axis=0)) * HD**-0.5)


def backward_kernel(
    index, dh_ref, u_ref, gain_ref, o_ref, lse_ref, sv, qx, wqkv_any, wout_any,
    du_ref, dgain_ref, dqkv_ref, dbr_ref,
    do_own, st_own, dob, stb, dox, stx, dk, dv, dqs, dkv_out, dqx, dq_far, landed,
    core_sem, st_sem, x_sem, stx_sem, dqx_sem, out_sem, local_sem, wqkv_ref, wout_ref, w_sem,
):
    place = lax.axis_index("dp")
    ex = lax.axis_index("expert")
    chip = place // 2
    core = lax.rem(place, 2)
    other = 1 - core
    half, width = u_ref.shape
    partner = (chip * 2 + other, ex)
    far = [((1 - chip) * 2 + t, ex) for t in range(2)]
    loads = [
        pltpu.make_async_copy(wout_any.at[index], wout_ref, w_sem.at[0]),
        pltpu.make_async_copy(wqkv_any.at[index], wqkv_ref, w_sem.at[1]),
    ]
    for load in loads:
        load.start()
    greet([partner] + far)
    dbr_ref[...] = dh_ref[...].astype(bfloat)
    loads[0].wait()
    do = mm(dbr_ref[...], wout_ref[...], NT).astype(bfloat)
    for p in range(6):
        do_own[p] = do[:, p * 128 : (p + 1) * 128]
    row = lax.broadcasted_iota(jnp.int32, (16, width), 0)
    head_of_row = (row // 8) * 6 + row % 8
    lane_head = lax.broadcasted_iota(jnp.int32, (16, width), 1) // HD
    picks = jnp.where(jnp.logical_and(head_of_row == lane_head, row % 8 < 6), 1.0, 0.0)
    deltas = lax.dot_general(
        picks,
        do.astype(single) * o_ref[...].astype(single),
        (NT, ((), ())),
        precision=highest,
        preferred_element_type=single,
    )
    for s in range(2):
        st_own[s, 0:8] = lse_ref[s]
        st_own[s, 8:16] = deltas[8 * s : 8 * s + 8]
    first = [
        send(st_own.at[other], stb.at[core], st_sem.at[0], st_sem.at[1], partner),
        send(do_own.at[pl.ds(other * 3, 3)], dob.at[:, core], core_sem.at[0], core_sem.at[1], partner),
        pltpu.make_async_copy(st_own.at[core], stb.at[core], local_sem.at[0]),
        pltpu.make_async_copy(do_own.at[pl.ds(core * 3, 3)], dob.at[:, core], local_sem.at[1]),
    ]
    for copy in first:
        copy.start()

    @pl.when(chip == 1)
    def _():
        for s in range(2):
            send(st_own.at[s], stx.at[core], stx_sem.at[0, s], stx_sem.at[1, core], far[s]).start()
        for p in range(3):
            for s in range(2):
                send(do_own.at[3 * s + p], dox.at[p, core], x_sem.at[0, p, s], x_sem.at[1, p, core], far[s]).start()

    dk[...] = jnp.zeros_like(dk)
    dv[...] = jnp.zeros_like(dv)
    for copy in first:
        copy.wait()

    def operands(p):
        keys = sv[1, p].reshape(2 * half, 128)
        keys_t = jnp.transpose(keys.astype(single)).astype(bfloat)
        return keys, keys_t, sv[2, p].reshape(2 * half, 128)

    step = half // 2

    def rows_of(j):
        return pl.ds((j % 2) * step, step)

    def stats_of(ref, p):
        def at(j):
            cols = slice((j % 2) * step, (j % 2 + 1) * step)
            lse = [ref[j // 2, pl.ds(2 * p + head, 1), cols] for head in range(2)]
            delta = [ref[j // 2, pl.ds(8 + 2 * p + head, 1), cols] for head in range(2)]
            return lse, delta

        return at

    def diagonal(p):
        keys, keys_t, values = operands(p)

        def put(j, grad):
            dqs[p, j // 2, rows_of(j)] = grad.astype(bfloat)

        pair_backward(
            lambda j: sv[0, p, j // 2, rows_of(j)],
            lambda j: dob[p, j // 2, rows_of(j)],
            stats_of(stb, p), keys, keys_t, values, True, put, (dk, dv, p), half,
        )

    diagonal(0)

    @pl.when(chip == 0)
    def _():
        for t in range(2):
            send(st_own.at[0], stx.at[t], stx_sem.at[0, t], stx_sem.at[1, t], partner).wait_recv()

        def cross(p, carry):
            for t in range(2):
                send(do_own.at[0], dox.at[p, t], x_sem.at[0, p, t], x_sem.at[1, p, t], partner).wait_recv()
            keys, keys_t, values = operands(p)

            def put(j, grad):
                dqx[p, j // 2, rows_of(j)] = grad.astype(bfloat)

            pair_backward(
                lambda j: qx[p, j // 2, rows_of(j)],
                lambda j: dox[p, j // 2, rows_of(j)],
                stats_of(stx, p), keys, keys_t, values, False, put, (dk, dv, p), half,
            )
            for t in range(2):
                send(dqx.at[p, t], dq_far.at[core * 3 + p], dqx_sem.at[0, p, t], dqx_sem.at[1, core * 3 + p, 0], far[t]).start()
            return carry

        lax.fori_loop(0, 3, cross, 0)

    for p in range(1, 3):
        diagonal(p)
    for p in range(3):
        for t in range(2):
            rows = slice(t * half, (t + 1) * half)
            dkv_out[t, 0, p] = dqs[p, t]
            dkv_out[t, 1, p] = dk[p, rows].astype(bfloat)
            dkv_out[t, 2, p] = dv[p, rows].astype(bfloat)
    last = send(dkv_out.at[other], landed, out_sem.at[0], out_sem.at[1], partner)
    last.start()
    last.wait()

    for i in range(3):
        for s in range(2):
            for p in range(3):
                part = jnp.where(s == core, dkv_out[core, i, p], landed[i, p])
                dqkv_ref[:, i * width + (3 * s + p) * 128 : i * width + (3 * s + p + 1) * 128] = part

    @pl.when(chip == 0)
    def _():
        for p in range(3):
            for t in range(2):
                send(dqx.at[p, t], dq_far.at[p], dqx_sem.at[0, p, t], dqx_sem.at[1, p, 0], far[t]).wait_send()

    @pl.when(chip == 1)
    def _():
        for s in range(2):
            send(st_own.at[s], stx.at[s], stx_sem.at[0, s], stx_sem.at[1, s], far[s]).wait_send()
        for p in range(3):
            for s in range(2):
                send(do_own.at[3 * s + p], dox.at[p, s], x_sem.at[0, p, s], x_sem.at[1, p, s], far[s]).wait_send()
        for s in range(2):
            for p in range(3):
                q = 3 * s + p
                send(dqx.at[p, s], dq_far.at[q], dqx_sem.at[0, p, s], dqx_sem.at[1, q, 0], far[s]).wait_recv()
                cols = slice(q * 128, (q + 1) * 128)
                dqkv_ref[:, cols] = (dqkv_ref[:, cols].astype(single) + dq_far[q].astype(single)).astype(bfloat)

    loads[1].wait()
    da = mm(dqkv_ref[...], wqkv_ref[...], NT)
    stream = u_ref[...]
    centered = stream - jnp.mean(stream, axis=-1, keepdims=True)
    factor = lax.rsqrt(jnp.mean(centered * centered, axis=-1, keepdims=True) + eps_norm)
    normed = centered * factor
    dgain_ref[...] = jnp.sum(da * normed, axis=0, keepdims=True)
    dn = da * gain_ref[2 * index : 2 * index + 1]
    inner = jnp.mean(dn * normed, axis=-1, keepdims=True)
    du_ref[...] = dh_ref[...] + factor * (dn - jnp.mean(dn, axis=-1, keepdims=True) - normed * inner)


def attention_backward_fast(upstream, saved, gains, w_qkv, w_out, index):
    stream, a, o, lse, sv, qx = saved
    rows, width = stream.shape
    dma, vm = pltpu.SemaphoreType.DMA, pltpu.VMEM
    tile = (rows, 128)
    outs = [((rows, width), single), ((1, width), single), ((rows, 3 * width), bfloat), ((rows, width), bfloat)]
    scratch = [
        vm((6,) + tile, bfloat),
        vm((2, 16, rows), single),
        vm((3, 2) + tile, bfloat),
        vm((2, 16, rows), single),
        vm((3, 2) + tile, bfloat),
        vm((2, 16, rows), single),
        vm((3, 2 * rows, 128), single),
        vm((3, 2 * rows, 128), single),
        vm((3, 2) + tile, bfloat),
        vm((2, 3, 3) + tile, bfloat),
        vm((3, 2) + tile, bfloat),
        vm((6,) + tile, bfloat),
        vm((3, 3) + tile, bfloat),
        dma((2,)),
        dma((2,)),
        dma((2, 3, 2)),
        dma((2, 2)),
        dma((2, 6, 2)),
        dma((2,)),
        dma((2,)),
        vm(w_qkv.shape[1:], bfloat),
        vm(w_out.shape[1:], bfloat),
        dma((2,)),
    ]
    du, dgain, dqkv, dbr = kernel_call(
        functools.partial(backward_kernel, index),
        outs,
        scratch,
        ("backward_zero", "backward_one")[index],
        60 * 10**9,
        (7, 8),
    )(upstream, stream, gains, o, lse, sv, qx, w_qkv, w_out)
    return du, dgain[0], dqkv, dbr


def flip_bits(place, bits, count):
    total = 0
    for i in range(count):
        bit = lax.rem(place // 2**i, 2)
        total = total + 2**i * (1 - bit if bits >> i & 1 else bit)
    return total


def core_sums(product, parts, landed, sems, partner, core, stay_ref, go_ref, axis):
    left, rights, shards, dense = product
    groups, unit = parts.shape[1], parts.shape[2]
    other = 1 - core
    block = 768
    deep = left.shape[1]
    per = deep // shards
    flipped = [jnp.transpose(left[:, first : first + block]) for first in range(0, deep, block)]
    pieces = []
    column = 0
    for right in rights:
        wide = right.shape[1]
        step = 768 if deep == block else 256
        pieces += [(right, start, column + start, step) for start in range(0, wide, step)]
        column += wide

    def finish(i):
        copies[i].wait()
        _, _, at, step = pieces[i]
        columns = slice(at, at + step)
        for g in range(groups // 2):
            for ref, pick in ((stay_ref, axis), (go_ref, 1 - axis)):
                spot = 2 * g + pick
                mine = parts[core, spot, :, columns].astype(single)
                ref[g, :, columns] = (mine + landed[spot, :, columns].astype(single)).astype(bfloat)

    copies = []
    for i, (right, start, at, step) in enumerate(pieces):
        for b, rows in enumerate(flipped):
            part = mm(rows, right[:, start : start + step]).astype(bfloat)
            for row in range(0, block, unit):
                shard, inside = (b * block + row) // per, (b * block + row) % per
                spot = (inside // unit, shard) if dense else (shard % 2, shard // 2)
                parts[spot[0], spot[1], :, at : at + step] = part[row : row + unit]
        columns = pl.ds(at, step)
        copy = send(parts.at[other, :, :, columns], landed.at[:, :, columns], sems.at[0, i], sems.at[1, i], partner)
        copy.start()
        copies.append(copy)
        if i >= 2:
            finish(i - 2)
    for i in range(max(0, len(pieces) - 2), len(pieces)):
        finish(i)


def weight_kernel(products, *refs):
    count = len(products)
    scratch = refs[-3 * count :]
    results = refs[-5 * count : -3 * count]
    place = lax.axis_index("dp")
    ex = lax.axis_index("expert")
    core = lax.rem(place, 2)
    partner = (place + 1 - 2 * core, ex)
    greet([partner])
    for i, (left, rights) in enumerate(products):
        parts, landed, sems = scratch[3 * i : 3 * i + 3]
        product = (refs[left], [refs[r] for r in rights], 8, True)
        core_sums(product, parts, landed, sems, partner, core, *results[2 * i : 2 * i + 2], lax.rem(ex, 2))


def sum_scratch(groups, unit, columns):
    return [
        pltpu.VMEM((2, groups, unit, columns), bfloat),
        pltpu.VMEM((groups, unit, columns), bfloat),
        pltpu.SemaphoreType.DMA((2, 4)),
    ]


def weight_products(products, sources, name):
    outs, scratch, flops = [], [], 0
    for left, rights in products:
        rows, deep = sources[left].shape
        columns = sum(sources[r].shape[1] for r in rights)
        outs += [((4, deep // 16, columns), bfloat)] * 2
        scratch += sum_scratch(8, deep // 16, columns)
        flops += 4 * rows * deep * columns
    return kernel_call(functools.partial(weight_kernel, products), outs, scratch, name, flops)(*sources)


def expert_kernel(
    rows_ref, row_target_ref, target_ref, scale_ref, count_ref, upstream_ref, up_any, down_any,
    result_ref, grad_ref, counts_ref, up_stay, up_go, down_stay, down_go,
    outgoing, scalars, arrived, scalars_in, acts, dhidden, dresult, back, back_in,
    up_parts, up_landed, up_sems, down_parts, down_landed, down_sems,
    up_ref, down_ref, load_sems, out_sems, scalar_sems, back_sems,
):
    place = lax.axis_index("dp")
    ex = lax.axis_index("expert")
    chip = place // 2
    core = lax.rem(place, 2)
    partner = (place + 1 - 2 * core, ex)
    experts, cap, width = arrived.shape
    loads = [
        pltpu.make_async_copy(up_any.at[0], up_ref, load_sems.at[0]),
        pltpu.make_async_copy(down_any.at[0], down_ref, load_sems.at[1]),
    ]
    for load in loads:
        load.start()
    far_first = (4, 5, 6, 7, 2, 3, 1)
    mates = {k: flip_bits(ex, k, 3) for k in far_first}
    greet([(place, mates[k]) for k in far_first] + [partner])
    tokens = rows_ref.shape[0]
    slots = experts * cap
    slot = lax.broadcasted_iota(jnp.int32, (slots, tokens), 0)
    picks = jnp.where(slot == row_target_ref[...], 1.0, 0.0).astype(bfloat)
    sent = mm(picks, rows_ref[...]).astype(bfloat)
    lane = lax.broadcasted_iota(jnp.int32, (tokens, 128), 1)
    for e in range(experts):
        outgoing[e] = sent[e * cap : (e + 1) * cap]
        here = jnp.logical_and(target_ref[...] == lane + e * cap, lane < cap)
        line = jnp.sum(jnp.where(here, scale_ref[...], 0.0), axis=0, keepdims=True)
        scalars[e] = jnp.concatenate([jnp.broadcast_to(line, (4, 128)), count_ref[0:4]], axis=0)
    for k in far_first:
        e = mates[k]
        send(scalars.at[e], scalars_in.at[ex], scalar_sems.at[0, k], scalar_sems.at[1, k], (place, e)).start()
        send(outgoing.at[e], arrived.at[ex], out_sems.at[0, k], out_sems.at[1, k], (place, e)).start()
    arrived[ex] = outgoing[ex]
    scalars_in[ex] = scalars[ex]
    for load in loads:
        load.wait()
    for i in range(4):
        for k in (2 * i, 2 * i + 1):
            if k:
                e = mates[k]
                send(scalars.at[e], scalars_in.at[e], scalar_sems.at[0, k], scalar_sems.at[1, k], (place, e)).wait()
                send(outgoing.at[e], arrived.at[e], out_sems.at[0, k], out_sems.at[1, k], (place, e)).wait()
        j = flip_bits(ex // 2, i, 2)
        rows = arrived[pl.ds(2 * j, 2)].reshape(2 * cap, width)
        for b in range(2):
            column = jnp.transpose(jnp.concatenate([scalars_in[2 * j + b]] * 16, axis=0))[:cap, 0:1]
            dresult[2 * j + b] = (upstream_ref[2 * j + b].astype(single) * column).astype(bfloat)
        upstream = dresult[pl.ds(2 * j, 2)].reshape(2 * cap, width)
        hidden_width = up_ref.shape[1]
        step = 768
        total = jnp.zeros((2 * cap, width), single)
        total_grad = jnp.zeros((2 * cap, width), single)
        for start in range(0, hidden_width, step):
            cols = slice(start, start + step)
            hidden = mm(rows, up_ref[:, cols])
            grad = mm(upstream, down_ref[cols, :], NT)
            square = hidden * hidden
            tanh = jnp.tanh(0.7978845608028654 * hidden * (1.0 + 0.044715 * square))
            act = (0.5 * hidden * (1.0 + tanh)).astype(bfloat)
            slope = 0.5 * (1.0 + tanh) + 0.5 * hidden * (1.0 - tanh * tanh) * (
                0.7978845608028654 * (1.0 + 3 * 0.044715 * square)
            )
            dhid = (grad * slope).astype(bfloat)
            acts[j, :, cols] = act
            dhidden[j, :, cols] = dhid
            total = total + mm(act, down_ref[cols, :])
            total_grad = total_grad + mm(dhid, up_ref[:, cols], NT)
        for b in range(2):
            back[0, 2 * j + b] = total_grad[b * cap : (b + 1) * cap].astype(bfloat)
            back[1, 2 * j + b] = total[b * cap : (b + 1) * cap].astype(bfloat)
        for k in (2 * i, 2 * i + 1):
            if k:
                e = mates[k]
                send(back.at[0, e], back_in.at[0, ex], back_sems.at[0, 0, k], back_sems.at[0, 1, k], (place, e)).start()
    for k in far_first:
        e = mates[k]
        send(back.at[1, e], back_in.at[1, ex], back_sems.at[1, 0, k], back_sems.at[1, 1, k], (place, e)).start()
    for half in range(2):
        back_in[half, ex] = back[half, ex]
    counts = scalars_in[0]
    for e in range(1, experts):
        counts = counts + scalars_in[e]
    counts_ref[...] = counts
    core_sums(
        (arrived.reshape(slots, width), [dhidden.reshape(slots, hidden_width)], 4, False),
        up_parts, up_landed, up_sems, partner, core, up_stay, up_go, chip,
    )
    core_sums(
        (acts.reshape(slots, hidden_width), [dresult.reshape(slots, width)], 4, False),
        down_parts, down_landed, down_sems, partner, core, down_stay, down_go, chip,
    )
    slot_lane = lax.broadcasted_iota(jnp.int32, (tokens, slots), 1)
    takes = jnp.where(target_ref[...] == slot_lane, 1.0, 0.0).astype(bfloat)
    for half, ref in ((0, grad_ref), (1, result_ref)):
        for k in far_first:
            e = mates[k]
            send(
                back.at[half, e], back_in.at[half, e], back_sems.at[half, 0, k], back_sems.at[half, 1, k], (place, e)
            ).wait()
        ref[...] = mm(takes, back_in[half].reshape(slots, width)).astype(bfloat)


def expert_layer(rows, target, scale, counts, upstream, w_up, w_down):
    tokens, width = rows.shape
    experts, cap = upstream.shape[:2]
    hidden = w_up.shape[2]
    dma, vm = pltpu.SemaphoreType.DMA, pltpu.VMEM
    block = (experts, cap, width)
    quarter = width // 4
    outs = [
        ((tokens, width), bfloat),
        ((tokens, width), bfloat),
        ((8, 128), single),
        ((1, quarter, hidden), bfloat),
        ((1, quarter, hidden), bfloat),
        ((1, hidden // 4, width), bfloat),
        ((1, hidden // 4, width), bfloat),
    ]
    scratch = [
        vm(block, bfloat),
        vm((experts, 8, 128), single),
        vm(block, bfloat),
        vm((experts, 8, 128), single),
        vm((4, 2 * cap, hidden), bfloat),
        vm((4, 2 * cap, hidden), bfloat),
        vm(block, bfloat),
        vm((2,) + block, bfloat),
        vm((2,) + block, bfloat),
        *sum_scratch(2, quarter, hidden),
        *sum_scratch(2, hidden // 4, width),
        vm(w_up.shape[1:], bfloat),
        vm(w_down.shape[1:], bfloat),
        dma((2,)),
        dma((2, 8)),
        dma((2, 8)),
        dma((2, 2, 8)),
    ]
    return kernel_call(expert_kernel, outs, scratch, "experts", 60 * 10**9, (6, 7), 60)(
        rows, target.reshape(1, tokens), target.reshape(tokens, 1), scale, counts, upstream, w_up, w_down
    )


def swap(array, axis_bit):
    expert = lax.axis_size("expert")
    total = lax.axis_size("dp") * expert
    step = expert << axis_bit if axis_bit < 2 else 1 << (axis_bit - 2)
    return lax.ppermute(array, ("dp", "expert"), [(i, i ^ step) for i in range(total)])


def added(left, right):
    return (left.astype(single) + right.astype(single)).astype(bfloat)


def pick(array, index, axis):
    return lax.dynamic_index_in_dim(array, index, axis, keepdims=False)


def sum_y(stay, go):
    return added(stay, swap(go, 2))


def sum_z(kept):
    z = lax.axis_index("expert") // 2
    kept = kept.reshape((2, 2) + kept.shape[1:])
    kept = added(pick(kept, z % 2, 1), swap(pick(kept, 1 - z % 2, 1), 3))
    return added(pick(kept, z // 2, 0), swap(pick(kept, 1 - z // 2, 0), 4))


def sum_x(kept):
    kept = added(kept, swap(kept, 1))
    mate = swap(kept, 0)
    core = lax.axis_index("dp") % 2
    first = jnp.where(core == 0, kept, mate).astype(single)
    second = jnp.where(core == 0, mate, kept).astype(single)
    return jnp.concatenate([first, second], axis=0)


def reduce_small(values):
    for bit in range(5):
        values = values + swap(values, bit)
    return values


def after(values, others):
    return lax.optimization_barrier((values, others))


def routing(expert_ids, expert_count, capacity):
    indices = expert_ids[:, 0]
    one_hot = (indices[:, None] == jnp.arange(expert_count, dtype=jnp.int32)[None, :]).astype(
        jnp.int32
    )
    earlier = jnp.cumsum(one_hot, axis=0) - one_hot
    slots = jnp.sum(earlier * one_hot, axis=1)
    kept_rows = slots < capacity
    target = jnp.where(kept_rows, indices * capacity + slots, expert_count * capacity)
    return (one_hot.astype(single), target, kept_rows)


def body_any(
    tokens,
    cotangent,
    expert_ids,
    loss_weights,
    section,
    norm_gains,
    attn_qkv,
    attn_out,
    ffn_up,
    ffn_down,
    expert_up,
    expert_down,
    router,
):
    row_count, model_width = tokens.shape
    expert_count = router.shape[1]
    capacity = 5 * row_count // (4 * expert_count)
    slots_all = expert_count * capacity
    group_count = lax.axis_size("expert")
    total_tokens = row_count * lax.axis_size("dp") * group_count
    offset = lax.axis_index("dp") * row_count
    sequence = lax.axis_index("expert")
    switch = section[sequence].astype(single)
    seq_weight = loss_weights[sequence].astype(single)
    inputs = tokens.astype(single)
    first_stream, saved_one = attention_forward(
        inputs, norm_gains[0], attn_qkv[0], attn_out[0], offset
    )
    ffn_out, ffn_normed, ffn_factor = norm_forward(first_stream, norm_gains[1])
    ffn_low = ffn_out.astype(bfloat)
    hidden = jnp.dot(ffn_low, ffn_up, preferred_element_type=single)
    acts_low = gelu_tanh(hidden).astype(bfloat)
    block_out = first_stream + jnp.dot(acts_low, ffn_down, preferred_element_type=single)
    second_stream, saved_two = attention_forward(
        block_out, norm_gains[2], attn_qkv[1], attn_out[1], offset
    )
    moe_in, moe_normed, moe_factor = norm_forward(second_stream, norm_gains[3])
    logits = jnp.dot(moe_in, router, precision=highest)
    one_hot, target, kept_rows = routing(expert_ids, expert_count, capacity)
    gates = jax.nn.sigmoid(jnp.sum(logits * one_hot, axis=1))
    outgoing = (
        jnp.zeros((slots_all, model_width), bfloat)
        .at[target]
        .set(moe_in.astype(bfloat), mode="drop")
    )
    arrived = lax.all_to_all(
        outgoing.reshape(expert_count, capacity, model_width),
        "expert",
        split_axis=0,
        concat_axis=0,
        tiled=True,
    )
    expert_rows = arrived.reshape(-1, model_width)
    expert_hidden = jnp.dot(expert_rows, expert_up[0], preferred_element_type=single)
    expert_acts = gelu_tanh(expert_hidden).astype(bfloat)
    expert_result = jnp.dot(expert_acts, expert_down[0], preferred_element_type=single).astype(
        bfloat
    )
    returned = lax.all_to_all(
        expert_result.reshape(group_count, capacity, model_width),
        "expert",
        split_axis=0,
        concat_axis=0,
        tiled=True,
    )
    safe_target = jnp.minimum(target, slots_all - 1)
    kept_float = kept_rows.astype(single)[:, None]
    moe_out = returned.reshape(slots_all, model_width)[safe_target].astype(single) * kept_float
    final = second_stream + gates[:, None] * moe_out
    counts, gate_sums = lax.psum(
        (jnp.sum(one_hot, axis=0), switch * jnp.sum(one_hot * gates[:, None], axis=0)),
        ("dp", "expert"),
    )
    mean_load = total_tokens / expert_count
    coef = (counts - mean_load) / mean_load
    load_balance = jnp.sum(coef * gate_sums) * (balance_rate / total_tokens)
    final_grad = cotangent.astype(single) * seq_weight
    gate_slope = gates * (1.0 - gates)
    gate_grad = jnp.sum(final_grad * moe_out, axis=1)
    balance_term = switch * (balance_rate / total_tokens) * jnp.sum(one_hot * coef[None, :], axis=1)
    logit_grad = (gate_grad + balance_term) * gate_slope
    result_grad = (final_grad * gates[:, None]).astype(bfloat)
    outgoing_grad = (
        jnp.zeros((slots_all, model_width), bfloat).at[target].set(result_grad, mode="drop")
    )
    grad_rows = lax.all_to_all(
        outgoing_grad.reshape(expert_count, capacity, model_width),
        "expert",
        split_axis=0,
        concat_axis=0,
        tiled=True,
    ).reshape(-1, model_width)
    down_expert_grad = jnp.dot(expert_acts.T, grad_rows, preferred_element_type=single)
    grad_acts = jnp.dot(grad_rows, expert_down[0].T, preferred_element_type=single)
    grad_hidden = gelu_back(expert_hidden, grad_acts).astype(bfloat)
    up_expert_grad = jnp.dot(expert_rows.T, grad_hidden, preferred_element_type=single)
    grad_inputs = jnp.dot(grad_hidden, expert_up[0].T, preferred_element_type=single).astype(bfloat)
    grad_back = lax.all_to_all(
        grad_inputs.reshape(group_count, capacity, model_width),
        "expert",
        split_axis=0,
        concat_axis=0,
        tiled=True,
    )
    moe_in_grad = grad_back.reshape(slots_all, model_width)[safe_target].astype(single) * kept_float
    routed_grad = logit_grad[:, None] * one_hot
    moe_in_grad = moe_in_grad + jnp.dot(routed_grad, router.T, precision=highest)
    router_local = switch * jnp.dot(moe_in.T, routed_grad, precision=highest)
    norm_grad_two, gain_three = norm_backward(moe_in_grad, moe_normed, moe_factor, norm_gains[3])
    second_grad = final_grad + norm_grad_two
    block_grad, gain_two, qkv_two, out_two = attention_backward(
        second_grad, saved_two, norm_gains[2], attn_qkv[1], attn_out[1], offset
    )
    branch_low = block_grad.astype(bfloat)
    down_local = jnp.dot(acts_low.T, branch_low, preferred_element_type=single)
    grad_dense_acts = jnp.dot(branch_low, ffn_down.T, preferred_element_type=single)
    grad_dense_hidden = gelu_back(hidden, grad_dense_acts).astype(bfloat)
    up_local = jnp.dot(ffn_low.T, grad_dense_hidden, preferred_element_type=single)
    ffn_in_grad = jnp.dot(grad_dense_hidden, ffn_up.T, preferred_element_type=single)
    norm_grad_one, gain_one = norm_backward(ffn_in_grad, ffn_normed, ffn_factor, norm_gains[1])
    first_grad = block_grad + norm_grad_one
    input_grad, gain_zero, qkv_one, out_one = attention_backward(
        first_grad, saved_one, norm_gains[0], attn_qkv[0], attn_out[0], offset
    )
    expert_up_part, expert_down_part = (
        lax.psum_scatter(
            up_expert_grad[None].astype(jnp.bfloat16), "dp", scatter_dimension=1, tiled=True
        ).astype(jnp.float32),
        lax.psum_scatter(
            down_expert_grad[None].astype(jnp.bfloat16), "dp", scatter_dimension=1, tiled=True
        ).astype(jnp.float32),
    )
    gains_local = jnp.stack([gain_zero, gain_one, gain_two, gain_three])
    gains_total, router_total = lax.psum((gains_local, router_local), ("dp", "expert"))
    qkv_local = jnp.stack([qkv_one, qkv_two])
    out_local = jnp.stack([out_one, out_two])
    qkv_part, out_part, up_part, down_part = (
        lax.psum_scatter(
            qkv_local.astype(jnp.bfloat16), "expert", scatter_dimension=1, tiled=True
        ).astype(jnp.float32),
        lax.psum_scatter(
            out_local.astype(jnp.bfloat16), "expert", scatter_dimension=1, tiled=True
        ).astype(jnp.float32),
        lax.psum_scatter(
            up_local.astype(jnp.bfloat16), "expert", scatter_dimension=0, tiled=True
        ).astype(jnp.float32),
        lax.psum_scatter(
            down_local.astype(jnp.bfloat16), "expert", scatter_dimension=0, tiled=True
        ).astype(jnp.float32),
    )
    qkv_part, out_part, up_part, down_part = (
        lax.psum(qkv_part.astype(jnp.bfloat16), "dp").astype(jnp.float32),
        lax.psum(out_part.astype(jnp.bfloat16), "dp").astype(jnp.float32),
        lax.psum(up_part.astype(jnp.bfloat16), "dp").astype(jnp.float32),
        lax.psum(down_part.astype(jnp.bfloat16), "dp").astype(jnp.float32),
    )
    return (
        block_out.astype(bfloat),
        final.astype(bfloat),
        input_grad,
        load_balance,
        gains_total,
        qkv_part,
        out_part,
        up_part,
        down_part,
        expert_up_part,
        expert_down_part,
        router_total,
    )


def body_fast(
    tokens,
    cotangent,
    expert_ids,
    loss_weights,
    section,
    norm_gains,
    attn_qkv,
    attn_out,
    ffn_up,
    ffn_down,
    expert_up,
    expert_down,
    router,
):
    row_count, model_width = tokens.shape
    expert_count = router.shape[1]
    capacity = 5 * row_count // (4 * expert_count)
    slots_all = expert_count * capacity
    group_count = lax.axis_size("expert")
    total_tokens = row_count * lax.axis_size("dp") * group_count
    sequence = lax.axis_index("expert")
    switch = section[sequence].astype(single)
    seq_weight = loss_weights[sequence].astype(single)
    one_hot, target, kept_rows = routing(expert_ids, expert_count, capacity)
    count_tile = jnp.zeros((8, 128), single).at[:, :expert_count].set(jnp.sum(one_hot, axis=0))
    slot_of = lax.broadcasted_iota(jnp.int32, (slots_all, row_count), 0) == target[None, :]
    upstream_slots = jnp.dot(slot_of.astype(bfloat), cotangent, preferred_element_type=single).astype(bfloat)
    upstream_slots = lax.all_to_all(
        upstream_slots.reshape(expert_count, capacity, model_width), "expert", split_axis=0, concat_axis=0, tiled=True
    )
    inputs = tokens.astype(single)
    first_stream, saved_one, _ = attention_forward_fast(inputs, norm_gains, attn_qkv, attn_out, count_tile, 0)
    ffn_out, ffn_normed, ffn_factor = norm_forward(first_stream, norm_gains[1])
    ffn_low = ffn_out.astype(bfloat)
    hidden = jnp.dot(ffn_low, ffn_up, preferred_element_type=single)
    acts_low = gelu_tanh(hidden).astype(bfloat)
    block_out = first_stream + jnp.dot(acts_low, ffn_down, preferred_element_type=single)
    second_stream, saved_two, count_tile = attention_forward_fast(
        block_out, norm_gains, attn_qkv, attn_out, count_tile, 1
    )
    moe_in, moe_normed, moe_factor = norm_forward(second_stream, norm_gains[3])
    logits = jnp.dot(moe_in, router, precision=highest)
    gates = jax.nn.sigmoid(jnp.sum(logits * one_hot, axis=1))
    moe_low, moe_grad_low, count_tile, up_stay, up_go, down_stay, down_go = expert_layer(
        moe_in.astype(bfloat),
        target,
        (gates * seq_weight)[:, None],
        count_tile,
        upstream_slots,
        expert_up,
        expert_down,
    )
    counts = count_tile[4, :expert_count]
    expert_up_part = up_stay.astype(single) + swap(up_go, 1).astype(single)
    expert_down_part = down_stay.astype(single) + swap(down_go, 1).astype(single)
    moe_out = moe_low.astype(single)
    final = second_stream + gates[:, None] * moe_out
    mean_load = total_tokens / expert_count
    coef = (counts - mean_load) / mean_load
    final_grad = cotangent.astype(single) * seq_weight
    gate_slope = gates * (1.0 - gates)
    gate_grad = jnp.sum(final_grad * moe_out, axis=1)
    balance_term = switch * (balance_rate / total_tokens) * jnp.sum(one_hot * coef[None, :], axis=1)
    logit_grad = (gate_grad + balance_term) * gate_slope
    routed_grad = logit_grad[:, None] * one_hot
    moe_in_grad = moe_grad_low.astype(single) + jnp.dot(routed_grad, router.T, precision=highest)
    router_local = switch * jnp.dot(moe_in.T, routed_grad, precision=highest)
    norm_grad_two, gain_three = norm_backward(moe_in_grad, moe_normed, moe_factor, norm_gains[3])
    second_grad = final_grad + norm_grad_two
    block_grad, gain_two, dqkv_two, dbr_two = attention_backward_fast(
        second_grad, saved_two, norm_gains, attn_qkv, attn_out, 1
    )
    products = ((0, (1,)), (2, (3,)))
    two = weight_products(
        products, [saved_two[1], dqkv_two, saved_two[2], dbr_two], "attention_weights_two"
    )
    block_grad, two = after(block_grad, two)
    branch_low = block_grad.astype(bfloat)
    grad_dense_acts = jnp.dot(branch_low, ffn_down.T, preferred_element_type=single)
    grad_dense_hidden = gelu_back(hidden, grad_dense_acts).astype(bfloat)
    ffn_in_grad = jnp.dot(grad_dense_hidden, ffn_up.T, preferred_element_type=single)
    up_halves = weight_products(((0, (1,)),), [ffn_low, grad_dense_hidden], "ffn_up_weights")
    down_halves = weight_products(((0, (1,)),), [acts_low, branch_low], "ffn_down_weights")
    norm_grad_one, gain_one = norm_backward(ffn_in_grad, ffn_normed, ffn_factor, norm_gains[1])
    first_grad = block_grad + norm_grad_one
    qkv_two, out_two = sum_y(*two[:2]), sum_y(*two[2:])
    first_grad, (up_halves, down_halves, qkv_two, out_two) = after(
        first_grad, (up_halves, down_halves, qkv_two, out_two)
    )
    gate_sums = switch * jnp.sum(one_hot * gates[:, None], axis=0)
    small = jnp.concatenate(
        [
            jnp.stack([gain_one, gain_two, gain_three]),
            router_local.T,
            jnp.pad(gate_sums, (0, model_width - expert_count))[None],
        ],
        axis=0,
    )
    small = reduce_small(small)
    input_grad, gain_zero, dqkv_one, dbr_one = attention_backward_fast(
        first_grad, saved_one, norm_gains, attn_qkv, attn_out, 0
    )
    one = weight_products(
        products, [saved_one[1], dqkv_one, saved_one[2], dbr_one], "attention_weights_one"
    )
    qkv_one, out_one = sum_x(sum_z(sum_y(*one[:2]))), sum_x(sum_z(sum_y(*one[2:])))
    qkv_two, out_two = sum_x(sum_z(qkv_two)), sum_x(sum_z(out_two))
    up_part, down_part = sum_x(sum_z(sum_y(*up_halves))), sum_x(sum_z(sum_y(*down_halves)))
    gain_zero = reduce_small(gain_zero[None])
    load_balance = jnp.sum(coef * small[3 + expert_count, :expert_count]) * (balance_rate / total_tokens)
    return (
        block_out.astype(bfloat),
        final.astype(bfloat),
        input_grad,
        load_balance,
        jnp.concatenate([gain_zero, small[:3]], axis=0),
        jnp.stack([qkv_one, qkv_two]),
        jnp.stack([out_one, out_two]),
        up_part,
        down_part,
        expert_up_part,
        expert_down_part,
        small[3 : 3 + expert_count].T,
    )


def solution(mesh):
    in_specs = (
        P(("dp", "expert"), None),
        P(("dp", "expert"), None),
        P(("dp", "expert"), None),
        P(),
        P(),
        P(),
        P(),
        P(),
        P(),
        P(),
        P("expert", None, None),
        P("expert", None, None),
        P(),
    )
    out_specs = (
        P(("dp", "expert"), None),
        P(("dp", "expert"), None),
        P(("dp", "expert"), None),
        P(),
        P(),
        P(None, "expert", None),
        P(None, "expert", None),
        P("expert", None),
        P("expert", None),
        P("expert", "dp", None),
        P("expert", "dp", None),
        P(),
    )
    shape = dict(mesh.shape)
    body = body_fast if shape["dp"] == 4 and shape["expert"] == 8 else body_any
    return jax.shard_map(body, mesh=mesh, in_specs=in_specs, out_specs=out_specs, check_vma=False)
```
